128 devices in a mesh: group: 8 (over y, core), shard: 16 (over z, x).
Axes of the slice: x: 4, y: 4, z: 4, core: 2. Of those that a mesh axis runs over, the one named last changes fastest.
Arguments:
- query_prefix: bfloat16 [2048, 256], P(('group', 'shard')), may hold values from -6 to 6
- query_tokens: bfloat16 [2048, 32, 128], P(('group', 'shard')), may hold values from -6 to 6
- probes: int32 [2048, 8], P(('group', 'shard')), may hold values from 0 to 63
- candidates: int32 [2048, 8], P(('group', 'shard')), may hold values from 0 to 32767, as said below
- passage_prefix: bfloat16 [32768, 256], P(('group', 'shard')), may hold values from -0.375 to 0.375
- passage_tokens: bfloat16 [32768, 128, 128], P(('group', 'shard')), may hold values from -0.5 to 0.5
Outputs:
- coarse: float32 [2048, 8], P(('group', 'shard'))
- rerank: float32 [2048, 8], P(('group', 'shard'))
The draws below stay inside these ranges and needn't reach their ends.
Inputs may be any that keep to these rules, and one draw needn't show every extreme that they name: `candidates`: for the 16 queries of one device (rows taken in aligned blocks of 16), at most 2 of their candidate entries lie among the 256 passages of any one device (passages of device d are d * 256 to (d + 1) * 256 - 1, devices numbered group first), and exactly 2 lie on some device.
All inputs are finite; a program needn't handle non-finite values.
Results may differ from the reference program's by a relative error of at most 0.00035.
Values may be sent and summed in bfloat16 or wider, within the bound.
A program may use at most 64 MiB of HBM per device.

```python
import jax
import jax.numpy as jnp
from jax import lax

PD = 256
TD = 128
LT = 128
QT = 32
CSIZE = 64
NPROBE = 8
NCAND = 8
Q_DEV = 16
CLUSTERS_PER_UNIT = 4
NQ = 2048
NP = 32768
CAP = 2
N_GROUP = 8
N_SHARD = 16


def draw_candidates(key, part):
    key = jax.random.fold_in(key, 11)
    devices = N_GROUP * N_SHARD
    slots = devices * CAP
    needed = Q_DEV * NCAND
    per_device = CLUSTERS_PER_UNIT * CSIZE

    def one_owner(owner_key):
        keys = jax.random.split(owner_key, 5)
        base = jax.random.permutation(keys[0], slots)
        offset = jax.random.randint(keys[1], (devices,), 0, slots)
        hottest = jax.random.randint(keys[2], (), 0, devices)
        slot_ids = jnp.arange(slots, dtype=jnp.int32)
        source = slot_ids // CAP
        score = (offset[source] + base) * slots + slot_ids
        score = jnp.where(source == hottest, slot_ids - slots, score)
        order = jnp.argsort(score, stable=True)
        chosen = order[:needed]
        chosen = chosen[jax.random.permutation(keys[3], needed)]
        within = jax.random.randint(keys[4], (needed,), 0, per_device)
        return (chosen // CAP * per_device + within).reshape(Q_DEV, NCAND).astype(jnp.int32)
    owner_keys = jax.random.split(key, devices)
    return jax.vmap(one_owner)(owner_keys).reshape(Q_DEV * devices, NCAND).astype(jnp.int32)


def set_ends(entries, key, low, top_value):
    longest = entries.shape.index(max(entries.shape))
    spots = []
    for shift in (0, 1):
        where = [jax.random.randint(jax.random.fold_in(key, axis), (), 0, length) for axis, length in enumerate(entries.shape)]
        where[longest] = (where[longest] + shift) % entries.shape[longest]
        spots.append(tuple(where))
    return entries.at[spots[0]].set(low).at[spots[1]].set(top_value)


def steps_of(rng, extent, cuts, low, top_value):
    factor_of = 1.0
    for position, shards_of in cuts:
        steps = jax.random.uniform(jax.random.fold_in(jax.random.fold_in(rng, 6), position), (shards_of,), jnp.float32, low / len(cuts), top_value / len(cuts))
        factor_of = factor_of * jnp.repeat(jnp.exp(steps), extent[position] // shards_of).reshape((-1,) + (1,) * (len(extent) - 1 - position))
    return factor_of


def normal_values(rng, extent, spread, most, shards=(), kind=jnp.bfloat16):
    level = steps_of(rng, extent, shards, -0.22, 0.18) if shards else 1.0
    entries = jax.random.normal(rng, extent, jnp.float32) * spread * level
    return jnp.minimum(jnp.maximum(entries, -most), most).astype(kind)


def setup_inputs(seed: int = 0) -> dict:
    key_list = jax.random.split(jax.random.key(seed), 7)
    query_prefix = normal_values(key_list[0], (NQ, PD), 1.0, 6.0, ((0, 128),))
    query_tokens = normal_values(key_list[1], (NQ, QT, TD), 1.0, 6.0, ((0, 128),))
    probes = set_ends(jax.random.randint(key_list[2], (NQ, NPROBE), 0, CLUSTERS_PER_UNIT * N_SHARD), jax.random.fold_in(key_list[2], 1), 0, (CLUSTERS_PER_UNIT * N_SHARD) - 1).astype(jnp.int32)
    candidates = draw_candidates(jax.random.fold_in(key_list[6], 71), 0)
    passage_prefix = normal_values(key_list[4], (NP, PD), PD ** -0.5, 0.375, ((0, 128),))
    passage_tokens = normal_values(key_list[5], (NP, LT, TD), TD ** -0.5, 0.5, ((0, 128),))
    return dict(query_prefix=query_prefix, query_tokens=query_tokens, probes=probes, candidates=candidates, passage_prefix=passage_prefix, passage_tokens=passage_tokens)


def reference(query_prefix, query_tokens, probes, candidates, passage_prefix, passage_tokens):
    devices = N_GROUP * N_SHARD
    group_clusters = CLUSTERS_PER_UNIT * N_SHARD

    def rough_block_scores(block):
        start = (block * Q_DEV).astype(jnp.int32)
        rows = lax.dynamic_slice_in_dim(query_prefix, start, Q_DEV, 0).astype(jnp.float32)
        probed = lax.dynamic_slice_in_dim(probes, start, Q_DEV, 0)
        group = (block // N_SHARD).astype(jnp.int32)
        clusters = group * group_clusters + probed
        passage_ids = (clusters[:, :, None] * CSIZE + jnp.arange(CSIZE, dtype=jnp.int32)[None, None, :]).astype(jnp.int32)
        prefixes = passage_prefix[passage_ids].astype(jnp.float32)
        scores = jnp.einsum('qd,qkcd->qkc', rows, prefixes)
        return jnp.max(scores, axis=-1)

    def rerank_block(block):
        start = (block * Q_DEV).astype(jnp.int32)
        token_matrix = lax.dynamic_slice_in_dim(query_tokens, start, Q_DEV, 0).astype(jnp.float32)
        listed = lax.dynamic_slice_in_dim(candidates, start, Q_DEV, 0)
        passage_texts = passage_tokens[listed].astype(jnp.float32)
        similarity_values = jnp.einsum('qtd,qcld->qctl', token_matrix, passage_texts)
        return jnp.mean(jnp.max(similarity_values, axis=-1), axis=-1)

    blocks = jnp.arange(devices, dtype=jnp.int32)
    coarse = lax.map(rough_block_scores, blocks).reshape(Q_DEV * devices, NPROBE)
    rerank = lax.map(rerank_block, blocks).reshape(Q_DEV * devices, NCAND)
    return (coarse, rerank)
```

```python
import functools

import jax
import jax.numpy as jnp
from jax import lax
from jax.experimental import pallas as pl
from jax.experimental.pallas import tpu as pltpu
from jax.sharding import PartitionSpec as P

CSIZE = 64
N_DEV = 128
N_GROUP = 8
N_SHARD = 16
BATCH = 8
N_BATCH = N_DEV // BATCH
MESH = pl.DeviceIdType.MESH


def offsets(j):
    a, b, c, d = j % 4, (j // 4) % 4, (j // 16) % 4, j // 64
    return (a + b + c) % 4, (d + a) % 2, (a + b) % 4, a


def kernel(
    qp_ref, qt_ref, probes_ref, cand_ref, pp_ref, pt_hbm,
    coarse_ref, rerank_ref,
    pt, stage, recv, all_qp, c_stage, c_recv, k_all, sel_v, r_stage, r_recv,
    sel_s, k_smem,
    pt_sem, loc_sem, send_sem, recv_sem, qp_send, qp_recv, ka_send, ka_recv,
    kb_send, kb_recv, c_send, c_rsem, r_send, r_rsem,
):
    g = lax.axis_index("group")
    s = lax.axis_index("shard")
    me = g * N_SHARD + s
    y, core, z, x = g // 2, g % 2, s // 4, s % 4

    def ahead(j):
        dy, dc, dz, dx = offsets(j)
        return ((y + dy) % 4) * 2 + (core + dc) % 2, ((z + dz) % 4) * 4 + (x + dx) % 4

    def behind(j):
        dy, dc, dz, dx = offsets(j)
        return ((y + 4 - dy) % 4) * 2 + (core + dc) % 2, ((z + 4 - dz) % 4) * 4 + (x + 4 - dx) % 4

    pt_copy = pltpu.make_async_copy(pt_hbm, pt, pt_sem)
    pt_copy.start()

    barrier = pltpu.get_barrier_semaphore()

    @pl.loop(1, N_DEV)
    def _(j):
        pl.semaphore_signal(barrier, inc=1, device_id=ahead(j), device_id_type=MESH)

    lane = lax.broadcasted_iota(jnp.int32, (16, 128), 1)
    row = lax.broadcasted_iota(jnp.int32, (16, 128), 0)
    cand = cand_ref[...]
    low = jnp.full((16, 128), 65536.0, jnp.float32)
    high = jnp.full((16, 128), -1.0, jnp.float32)
    for k in range(8):
        c = cand[:, k : k + 1]
        key = ((row * 8 + k) * 256 + (c & 255)).astype(jnp.float32)
        hit = (c >> 8) == lane
        low = jnp.minimum(low, jnp.where(hit, key, 65536.0))
        high = jnp.maximum(high, jnp.where(hit, key, -1.0))
    low = jnp.min(low, axis=0, keepdims=True)
    high = jnp.max(high, axis=0, keepdims=True)
    used = high >= 0.0
    low_i = jnp.where(used, low, 0.0).astype(jnp.int32)
    high_i = jnp.where(used, high, 0.0).astype(jnp.int32)
    sel_v[...] = (low_i >> 11) + (high_i >> 11) * 16
    k_all[me] = (low_i & 255) + (high_i & 255) * 256
    first_flat = low_i >> 8

    sel_copy = pltpu.make_async_copy(sel_v, sel_s, loc_sem)
    sel_copy.start()
    sel_copy.wait()

    v = sel_s[0, me]
    recv[0, 0] = qt_ref[v & 15]
    recv[0, 1] = qt_ref[(v >> 4) & 15]

    @pl.loop(1, N_DEV)
    def _(j):
        dg, ds = ahead(j)
        v = sel_s[0, dg * N_SHARD + ds]
        stage[j, 0] = qt_ref[v & 15]
        stage[j, 1] = qt_ref[(v >> 4) & 15]

    all_qp[s] = qp_ref[...]

    pl.semaphore_wait(barrier, N_DEV - 1)

    @pl.loop(1, N_SHARD)
    def _(i):
        mate = (s + i) % N_SHARD
        pltpu.make_async_remote_copy(
            k_all.at[me], k_all.at[me], ka_send, ka_recv, (g, mate), MESH
        ).start()
        pltpu.make_async_remote_copy(
            qp_ref, all_qp.at[s], qp_send, qp_recv, (g, mate), MESH
        ).start()

    def send_tokens(j):
        pltpu.make_async_remote_copy(
            stage.at[j], recv.at[j], send_sem, recv_sem.at[j // BATCH], ahead(j), MESH
        ).start()

    @pl.loop(1, 32)
    def _(j):
        send_tokens(j)

    pltpu.make_async_copy(k_all.at[pl.ds(0, 15)], k_all.at[pl.ds(0, 15)], ka_recv).wait()

    @pl.loop(1, N_GROUP)
    def _(i):
        rows = k_all.at[pl.ds(g * N_SHARD, N_SHARD)]
        pltpu.make_async_remote_copy(
            rows, rows, kb_send, kb_recv, ((g + i) % N_GROUP, s), MESH
        ).start()

    @pl.loop(32, N_DEV)
    def _(j):
        send_tokens(j)

    pltpu.make_async_copy(all_qp.at[pl.ds(0, 15)], all_qp.at[pl.ds(0, 15)], qp_recv).wait()
    scores = lax.dot_general(
        all_qp[...].reshape(256, 256), pp_ref[...], (((1,), (1,)), ((), ())),
        preferred_element_type=jnp.float32,
    )
    lane2 = lax.broadcasted_iota(jnp.int32, (256, 128), 1)
    best = jnp.zeros((256, 128), jnp.float32)
    for c in range(4):
        half = scores[:, 128 * (c // 2) : 128 * (c // 2) + 128]
        top = jnp.max(jnp.where(lane2 // CSIZE == c % 2, half, -jnp.inf), axis=1, keepdims=True)
        best = jnp.where(lane2 == 4 * s + c, top, best)
    c_stage[...] = best.reshape(16, 16, 128)
    c_recv[s] = c_stage[s]

    @pl.loop(1, N_SHARD)
    def _(i):
        mate = (s + i) % N_SHARD
        pltpu.make_async_remote_copy(
            c_stage.at[mate], c_recv.at[s], c_send, c_rsem, (g, mate), MESH
        ).start()

    pltpu.make_async_copy(k_all.at[pl.ds(0, 112)], k_all.at[pl.ds(0, 112)], kb_recv).wait()
    k_copy = pltpu.make_async_copy(k_all, k_smem, loc_sem)
    k_copy.start()
    k_copy.wait()
    pt_copy.wait()

    lane_r = lax.broadcasted_iota(jnp.int32, (2, 128), 1)

    def score(j):
        bg, bs = behind(j)
        w = k_smem[bg * N_SHARD + bs, 0, me]
        tops = []
        for slot, i in ((0, w & 255), (1, (w >> 8) & 255)):
            sim = lax.dot_general(
                pt[i], recv[j, slot], (((1,), (1,)), ((), ())), preferred_element_type=jnp.float32
            )
            tops.append(jnp.max(sim, axis=0, keepdims=True))
        mean = jnp.sum(jnp.concatenate(tops, axis=0), axis=1, keepdims=True) * (1.0 / 32)
        return jnp.where(lane_r == me, mean, 0.0)

    def back(j):
        pltpu.make_async_remote_copy(
            r_stage.at[j], r_recv.at[j], r_send, r_rsem, behind(j), MESH
        ).start()

    pltpu.make_async_copy(recv.at[pl.ds(1, 7)], recv.at[pl.ds(1, 7)], recv_sem.at[0]).wait()
    r_recv[0] = score(0)
    for j in range(1, BATCH):
        r_stage[j] = score(j)
        back(j)

    @pl.loop(1, N_BATCH)
    def _(b):
        pltpu.make_async_copy(
            recv.at[pl.ds(b * BATCH, BATCH)], recv.at[pl.ds(b * BATCH, BATCH)], recv_sem.at[b]
        ).wait()
        for t in range(BATCH):
            r_stage[b * BATCH + t] = score(b * BATCH + t)
        for t in range(BATCH):
            back(b * BATCH + t)

    lane8 = lax.broadcasted_iota(jnp.int32, (16, 8), 1)

    pltpu.make_async_copy(c_recv.at[pl.ds(0, 15)], c_recv.at[pl.ds(0, 15)], c_rsem).wait()
    all_best = jnp.sum(c_recv[...], axis=0)
    probes = probes_ref[...]
    out = jnp.zeros((16, 8), jnp.float32)
    for k in range(8):
        pick = jnp.sum(jnp.where(probes[:, k : k + 1] == lane, all_best, 0.0), axis=1, keepdims=True)
        out = jnp.where(lane8 == k, pick, out)
    coarse_ref[...] = out

    pltpu.make_async_copy(r_recv.at[pl.ds(1, 127)], r_recv.at[pl.ds(1, 127)], r_rsem).wait()
    both = jnp.sum(r_recv[...], axis=0)
    out = jnp.zeros((16, 8), jnp.float32)
    for k in range(8):
        here = (cand[:, k : k + 1] >> 8) == lane
        value = jnp.where(first_flat == row * 8 + k, both[0:1], both[1:2])
        pick = jnp.sum(jnp.where(here, value, 0.0), axis=1, keepdims=True)
        out = jnp.where(lane8 == k, pick, out)
    rerank_ref[...] = out

    def sent(ref, sem):
        pltpu.make_async_copy(ref, ref, sem).wait()

    sent(stage.at[pl.ds(1, 127)], send_sem)
    sent(all_qp.at[pl.ds(0, 15)], qp_send)
    sent(k_all.at[pl.ds(0, 15)], ka_send)
    sent(k_all.at[pl.ds(0, 112)], kb_send)
    sent(c_recv.at[pl.ds(0, 15)], c_send)
    sent(r_stage.at[pl.ds(1, 127)], r_send)


def body(query_prefix, query_tokens, probes, candidates, passage_prefix, passage_tokens):
    vmem = pl.BlockSpec(memory_space=pltpu.VMEM)
    dma = pltpu.SemaphoreType.DMA
    return tuple(
        pl.pallas_call(
            kernel,
            out_shape=(
                jax.ShapeDtypeStruct((16, 8), jnp.float32),
                jax.ShapeDtypeStruct((16, 8), jnp.float32),
            ),
            in_specs=[vmem] * 5 + [pl.BlockSpec(memory_space=pltpu.HBM)],
            out_specs=(vmem, vmem),
            scratch_shapes=[
                pltpu.VMEM((256, 128, 128), jnp.bfloat16),
                pltpu.VMEM((N_DEV, 2, 32, 128), jnp.bfloat16),
                pltpu.VMEM((N_DEV, 2, 32, 128), jnp.bfloat16),
                pltpu.VMEM((16, 16, 256), jnp.bfloat16),
                pltpu.VMEM((16, 16, 128), jnp.float32),
                pltpu.VMEM((16, 16, 128), jnp.float32),
                pltpu.VMEM((N_DEV, 1, 128), jnp.int32),
                pltpu.VMEM((1, 128), jnp.int32),
                pltpu.VMEM((N_DEV, 2, 128), jnp.float32),
                pltpu.VMEM((N_DEV, 2, 128), jnp.float32),
                pltpu.SMEM((1, 128), jnp.int32),
                pltpu.SMEM((N_DEV, 1, 128), jnp.int32),
                dma, dma, dma, dma((N_BATCH,)), dma, dma, dma, dma, dma, dma, dma, dma, dma, dma,
            ],
            compiler_params=pltpu.CompilerParams(
                collective_id=0, has_side_effects=True, vmem_limit_bytes=48 * 1024 * 1024
            ),
            cost_estimate=pl.CostEstimate(
                flops=300_000_000, bytes_accessed=8_700_000, transcendentals=0
            ),
        )(query_prefix, query_tokens, probes, candidates, passage_prefix, passage_tokens)
    )


def solution(mesh):
    both = ("group", "shard")
    flat, cube = P(both, None), P(both, None, None)
    return jax.shard_map(
        body,
        mesh=mesh,
        in_specs=(flat, cube, flat, flat, flat, cube),
        out_specs=(flat, flat),
        check_vma=False,
    )
```

```python
import functools

import jax
import jax.numpy as jnp
from jax import lax
from jax.experimental import pallas as pl
from jax.experimental.pallas import tpu as pltpu
from jax.sharding import PartitionSpec as P

CSIZE = 64
N_DEV = 128
N_GROUP = 8
N_SHARD = 16
BATCH = 8
N_BATCH = N_DEV // BATCH
SPLIT = 64
MESH = pl.DeviceIdType.MESH


def offsets(j):
    a, b, c = (j // 2) % 4, (j // 8) % 4, j // 32
    return (a + b + c) % 4, j % 2, (a + b) % 4, a


def place(dy, dc, dz, dx):
    return (((dy + 4 - dz) % 4 * 4 + (dz + 4 - dx) % 4) * 4 + dx) * 2 + dc


def kernel(
    qp_hbm, qt_hbm, probes_hbm, cand_hbm, pp_hbm, pt_hbm,
    coarse_ref, rerank_ref,
    qp_ref, qt_ref, probes_ref, cand_ref, pp_ref, pt, stage, recv, all_qp, c_stage, c_recv, k_all, sel_v, r_stage, r_recv,
    sel_s, k_smem,
    in_sem, loc_sem, ready_sem, send_sem, recv_sem, qp_send, qp_recv, ka_send, ka_recv,
    kb_send, kb_recv, c_send, c_rsem, r_send, r_rsem,
):
    g = lax.axis_index("group")
    s = lax.axis_index("shard")
    me = g * N_SHARD + s
    y, core, z, x = g // 2, g % 2, s // 4, s % 4

    def ahead(j):
        dy, dc, dz, dx = offsets(j)
        return ((y + dy) % 4) * 2 + (core + dc) % 2, ((z + dz) % 4) * 4 + (x + dx) % 4

    def behind(j):
        dy, dc, dz, dx = offsets(j)
        return ((y + 4 - dy) % 4) * 2 + (core + dc) % 2, ((z + 4 - dz) % 4) * 4 + (x + 4 - dx) % 4

    barrier = pltpu.get_barrier_semaphore()

    @pl.loop(1, N_SHARD)
    def _(i):
        pl.semaphore_signal(
            barrier, inc=1, device_id=(g, (s + i) % N_SHARD), device_id_type=MESH
        )

    @pl.loop(1, N_GROUP)
    def _(i):
        pl.semaphore_signal(
            barrier, inc=1, device_id=((g + i) % N_GROUP, s), device_id_type=MESH
        )

    loads = [
        pltpu.make_async_copy(src, dst, in_sem.at[i])
        for i, (src, dst) in enumerate(
            [(cand_hbm, cand_ref), (qt_hbm, qt_ref), (qp_hbm, qp_ref), (probes_hbm, probes_ref),
             (pp_hbm, pp_ref), (pt_hbm, pt)]
        )
    ]
    for load in loads:
        load.start()
    cand_load, qt_load, qp_load, probes_load, pp_load, pt_load = loads

    lane = lax.broadcasted_iota(jnp.int32, (16, 128), 1)
    row = lax.broadcasted_iota(jnp.int32, (16, 128), 0)
    eye = lax.broadcasted_iota(jnp.int32, (16, 16), 0) == lax.broadcasted_iota(jnp.int32, (16, 16), 1)

    def columns(ref):
        table = ref[...].astype(jnp.float32)
        return [
            jnp.sum(jnp.where(eye, table[k : k + 1], 0.0), axis=1, keepdims=True).astype(jnp.int32)
            for k in range(8)
        ]

    cand_load.wait()
    cand = columns(cand_ref)
    low = jnp.full((16, 128), 65536.0, jnp.float32)
    high = jnp.full((16, 128), -1.0, jnp.float32)
    for k in range(8):
        c = cand[k]
        key = ((row * 8 + k) * 256 + (c & 255)).astype(jnp.float32)
        hit = (c >> 8) == lane
        low = jnp.minimum(low, jnp.where(hit, key, 65536.0))
        high = jnp.maximum(high, jnp.where(hit, key, -1.0))
    low = jnp.min(low, axis=0, keepdims=True)
    high = jnp.max(high, axis=0, keepdims=True)
    used = high >= 0.0
    low_i = jnp.where(used, low, 0.0).astype(jnp.int32)
    high_i = jnp.where(used, high, 0.0).astype(jnp.int32)
    sel_v[...] = (low_i >> 11) + (high_i >> 11) * 16
    k_all[me] = (low_i & 255) + (high_i & 255) * 256
    first_flat = low_i >> 8

    sel_copy = pltpu.make_async_copy(sel_v, sel_s, loc_sem)
    sel_copy.start()
    sel_copy.wait()

    qt_load.wait()
    v = sel_s[0, me]
    recv[0, 0] = qt_ref[v & 15]
    recv[0, 1] = qt_ref[(v >> 4) & 15]

    @pl.loop(1, N_DEV)
    def _(j):
        dg, ds = ahead(j)
        v = sel_s[0, dg * N_SHARD + ds]
        stage[j, 0] = qt_ref[v & 15]
        stage[j, 1] = qt_ref[(v >> 4) & 15]

    qp_load.wait()
    all_qp[s] = qp_ref[...]

    pl.semaphore_wait(barrier, N_SHARD + N_GROUP - 2)

    @pl.loop(1, N_GROUP)
    def _(i):
        pl.semaphore_signal(
            ready_sem, inc=1, device_id=((g + i) % N_GROUP, s), device_id_type=MESH
        )

    @pl.loop(1, N_SHARD)
    def _(i):
        pltpu.make_async_remote_copy(
            k_all.at[me], k_all.at[me], ka_send, ka_recv, (g, (s + i) % N_SHARD), MESH
        ).start()

    def send_tokens(j):
        pltpu.make_async_remote_copy(
            stage.at[j], recv.at[j], send_sem, recv_sem.at[j // BATCH], ahead(j), MESH
        ).start()

    def send_far(j):
        dy, dc, dz, dx = offsets(j)

        @pl.when(jnp.logical_and(dy + dc > 0, dz + dx > 0))
        def _():
            send_tokens(j)

    @pl.loop(1, N_SHARD)
    def _(i):
        send_tokens(place(0, 0, i // 4, i % 4))

    @pl.loop(1, N_GROUP)
    def _(i):
        send_tokens(place(i // 2, i % 2, 0, 0))

    pltpu.make_async_copy(k_all.at[pl.ds(0, 15)], k_all.at[pl.ds(0, 15)], ka_recv).wait()

    @pl.loop(1, N_GROUP)
    def _(i):
        rows = k_all.at[pl.ds(g * N_SHARD, N_SHARD)]
        pltpu.make_async_remote_copy(
            rows, rows, kb_send, kb_recv, ((g + i) % N_GROUP, s), MESH
        ).start()

    @pl.loop(1, N_SHARD)
    def _(i):
        pltpu.make_async_remote_copy(
            qp_ref, all_qp.at[s], qp_send, qp_recv, (g, (s + i) % N_SHARD), MESH
        ).start()

    pl.semaphore_wait(ready_sem, N_GROUP - 1)
    pl.loop(1, SPLIT)(send_far)

    pltpu.make_async_copy(k_all.at[pl.ds(0, 112)], k_all.at[pl.ds(0, 112)], kb_recv).wait()
    k_copy = pltpu.make_async_copy(k_all, k_smem, loc_sem)
    k_copy.start()
    k_copy.wait()
    pl.loop(SPLIT, N_DEV)(send_far)

    pp_load.wait()

    pltpu.make_async_copy(all_qp.at[pl.ds(0, 15)], all_qp.at[pl.ds(0, 15)], qp_recv).wait()
    scores = lax.dot_general(
        all_qp[...].reshape(256, 256), pp_ref[...], (((1,), (1,)), ((), ())),
        preferred_element_type=jnp.float32,
    )
    lane2 = lax.broadcasted_iota(jnp.int32, (256, 128), 1)
    best = jnp.zeros((256, 128), jnp.float32)
    for c in range(4):
        half = scores[:, 128 * (c // 2) : 128 * (c // 2) + 128]
        top = jnp.max(jnp.where(lane2 // CSIZE == c % 2, half, -jnp.inf), axis=1, keepdims=True)
        best = jnp.where(lane2 == 4 * s + c, top, best)
    c_stage[...] = best.reshape(16, 16, 128)
    c_recv[s] = c_stage[s]

    @pl.loop(1, N_SHARD)
    def _(i):
        mate = (s + i) % N_SHARD
        pltpu.make_async_remote_copy(
            c_stage.at[mate], c_recv.at[s], c_send, c_rsem, (g, mate), MESH
        ).start()

    pt_load.wait()

    lane_r = lax.broadcasted_iota(jnp.int32, (2, 128), 1)
    own = lax.broadcasted_iota(jnp.int32, (2, 64), 1) // 32 == lax.broadcasted_iota(
        jnp.int32, (2, 64), 0
    )
    none = jnp.zeros((32, 128), jnp.bfloat16)

    def score(j):
        bg, bs = behind(j)
        w = k_smem[bg * N_SHARD + bs, 0, me]
        texts = jnp.concatenate([pt[w & 255], pt[(w >> 8) & 255]], axis=1)
        tokens = jnp.concatenate(
            [
                jnp.concatenate([recv[j, 0], none], axis=1),
                jnp.concatenate([none, recv[j, 1]], axis=1),
            ],
            axis=0,
        )
        sim = lax.dot_general(
            texts, tokens, (((1,), (1,)), ((), ())), preferred_element_type=jnp.float32
        )
        top = jnp.max(sim, axis=0, keepdims=True)
        mean = jnp.sum(jnp.where(own, top, 0.0), axis=1, keepdims=True) * (1.0 / 32)
        return jnp.where(lane_r == me, mean, 0.0)

    def back(j):
        pltpu.make_async_remote_copy(
            r_stage.at[j], r_recv.at[j], r_send, r_rsem, behind(j), MESH
        ).start()

    pltpu.make_async_copy(recv.at[pl.ds(1, 7)], recv.at[pl.ds(1, 7)], recv_sem.at[0]).wait()
    r_recv[0] = score(0)
    for j in range(1, BATCH):
        r_stage[j] = score(j)
        back(j)

    @pl.loop(1, N_BATCH)
    def _(b):
        pltpu.make_async_copy(
            recv.at[pl.ds(b * BATCH, BATCH)], recv.at[pl.ds(b * BATCH, BATCH)], recv_sem.at[b]
        ).wait()
        for t in range(BATCH):
            r_stage[b * BATCH + t] = score(b * BATCH + t)
        for t in range(BATCH):
            back(b * BATCH + t)

    lane8 = lax.broadcasted_iota(jnp.int32, (16, 8), 1)

    pltpu.make_async_copy(c_recv.at[pl.ds(0, 15)], c_recv.at[pl.ds(0, 15)], c_rsem).wait()
    probes_load.wait()
    all_best = jnp.sum(c_recv[...], axis=0)
    probes = columns(probes_ref)
    out = jnp.zeros((16, 8), jnp.float32)
    for k in range(8):
        pick = jnp.sum(jnp.where(probes[k] == lane, all_best, 0.0), axis=1, keepdims=True)
        out = jnp.where(lane8 == k, pick, out)
    coarse_ref[...] = out

    pltpu.make_async_copy(r_recv.at[pl.ds(1, 127)], r_recv.at[pl.ds(1, 127)], r_rsem).wait()
    both = jnp.sum(r_recv[...], axis=0)
    out = jnp.zeros((16, 8), jnp.float32)
    for k in range(8):
        here = (cand[k] >> 8) == lane
        value = jnp.where(first_flat == row * 8 + k, both[0:1], both[1:2])
        pick = jnp.sum(jnp.where(here, value, 0.0), axis=1, keepdims=True)
        out = jnp.where(lane8 == k, pick, out)
    rerank_ref[...] = out

    def sent(ref, sem):
        pltpu.make_async_copy(ref, ref, sem).wait()

    sent(stage.at[pl.ds(1, 127)], send_sem)
    sent(all_qp.at[pl.ds(0, 15)], qp_send)
    sent(k_all.at[pl.ds(0, 15)], ka_send)
    sent(k_all.at[pl.ds(0, 112)], kb_send)
    sent(c_recv.at[pl.ds(0, 15)], c_send)
    sent(r_stage.at[pl.ds(1, 127)], r_send)


def body(query_prefix, query_tokens, probes, candidates, passage_prefix, passage_tokens):
    vmem = pl.BlockSpec(memory_space=pltpu.VMEM)
    dma = pltpu.SemaphoreType.DMA
    return tuple(
        pl.pallas_call(
            kernel,
            out_shape=(
                jax.ShapeDtypeStruct((16, 8), jnp.float32),
                jax.ShapeDtypeStruct((16, 8), jnp.float32),
            ),
            in_specs=[pl.BlockSpec(memory_space=pltpu.HBM)] * 6,
            out_specs=(vmem, vmem),
            scratch_shapes=[
                pltpu.VMEM((16, 256), jnp.bfloat16),
                pltpu.VMEM((16, 32, 128), jnp.bfloat16),
                pltpu.VMEM((8, 16), jnp.int32),
                pltpu.VMEM((8, 16), jnp.int32),
                pltpu.VMEM((256, 256), jnp.bfloat16),
                pltpu.VMEM((256, 128, 128), jnp.bfloat16),
                pltpu.VMEM((N_DEV, 2, 32, 128), jnp.bfloat16),
                pltpu.VMEM((N_DEV, 2, 32, 128), jnp.bfloat16),
                pltpu.VMEM((16, 16, 256), jnp.bfloat16),
                pltpu.VMEM((16, 16, 128), jnp.float32),
                pltpu.VMEM((16, 16, 128), jnp.float32),
                pltpu.VMEM((N_DEV, 1, 128), jnp.int32),
                pltpu.VMEM((1, 128), jnp.int32),
                pltpu.VMEM((N_DEV, 2, 128), jnp.float32),
                pltpu.VMEM((N_DEV, 2, 128), jnp.float32),
                pltpu.SMEM((1, 128), jnp.int32),
                pltpu.SMEM((N_DEV, 1, 128), jnp.int32),
                dma((6,)), dma, pltpu.SemaphoreType.REGULAR,
                dma, dma((N_BATCH,)), dma, dma, dma, dma, dma, dma, dma, dma, dma, dma,
            ],
            compiler_params=pltpu.CompilerParams(
                collective_id=0, has_side_effects=True, vmem_limit_bytes=60 * 1024 * 1024
            ),
            cost_estimate=pl.CostEstimate(
                flops=300_000_000, bytes_accessed=8_700_000, transcendentals=0
            ),
        )(query_prefix, query_tokens, probes.T, candidates.T, passage_prefix, passage_tokens)
    )


def solution(mesh):
    both = ("group", "shard")
    flat, cube = P(both, None), P(both, None, None)
    return jax.shard_map(
        body,
        mesh=mesh,
        in_specs=(flat, cube, flat, flat, flat, cube),
        out_specs=(flat, flat),
        check_vma=False,
    )
```

```python
import functools

import jax
import jax.numpy as jnp
from jax import lax
from jax.experimental import pallas as pl
from jax.experimental.pallas import tpu as pltpu
from jax.sharding import PartitionSpec as P

CSIZE = 64
N_DEV = 128
N_GROUP = 8
N_SHARD = 16
BATCH = 16
HALF = BATCH // 2
LEAD = 16
N_BATCH = N_DEV // BATCH
MESH = pl.DeviceIdType.MESH


def mod4(n):
    return lax.rem(n, 4)


def offsets(j):
    a, b, c = mod4(lax.div(j, 2)), mod4(lax.div(j, 8)), lax.div(j, 32)
    return mod4(a + b + c), lax.rem(j, 2), mod4(a + b), a


def place(dy, dc, dz, dx):
    return ((mod4(dy + 4 - dz) * 4 + mod4(dz + 4 - dx)) * 4 + dx) * 2 + dc


def kernel(
    qp_hbm, qt_hbm, probes_hbm, cand_hbm, pp_hbm, pt_hbm,
    coarse_ref, rerank_ref,
    qp_ref, qt_ref, probes_ref, cand_ref, pp_ref, pt, stage, recv, all_qp, c_stage, c_recv, sel_v, key_v, k_all, r_stage, r_recv,
    sel_s, k_smem,
    in_sem, loc_sem, k_sem, ready_sem, send_sem, recv_sem, qp_send, qp_recv, k_send, k_recv,
    c_send, c_rsem, r_send, r_rsem,
):
    g = lax.axis_index("group")
    s = lax.axis_index("shard")
    me = g * N_SHARD + s
    y, core, z, x = g // 2, g % 2, s // 4, s % 4

    def ahead(j):
        dy, dc, dz, dx = offsets(j)
        return mod4(y + dy) * 2 + lax.rem(core + dc, 2), mod4(z + dz) * 4 + mod4(x + dx)

    def behind(j):
        dy, dc, dz, dx = offsets(j)
        return mod4(y + 4 - dy) * 2 + lax.rem(core + dc, 2), mod4(z + 4 - dz) * 4 + mod4(x + 4 - dx)

    barrier = pltpu.get_barrier_semaphore()

    @pl.loop(1, N_SHARD)
    def _(i):
        pl.semaphore_signal(
            barrier, inc=1, device_id=(g, (s + i) % N_SHARD), device_id_type=MESH
        )

    @pl.loop(1, N_GROUP)
    def _(i):
        pl.semaphore_signal(
            barrier, inc=1, device_id=((g + i) % N_GROUP, s), device_id_type=MESH
        )

    loads = [
        pltpu.make_async_copy(src, dst, in_sem.at[i])
        for i, (src, dst) in enumerate(
            [(cand_hbm, cand_ref), (qt_hbm, qt_ref), (qp_hbm, qp_ref), (probes_hbm, probes_ref),
             (pp_hbm, pp_ref), (pt_hbm, pt)]
        )
    ]
    for load in loads:
        load.start()
    cand_load, qt_load, qp_load, probes_load, pp_load, pt_load = loads

    lane = lax.broadcasted_iota(jnp.int32, (16, 128), 1)
    row = lax.broadcasted_iota(jnp.int32, (16, 128), 0)
    eye = lax.broadcasted_iota(jnp.int32, (16, 16), 0) == lax.broadcasted_iota(jnp.int32, (16, 16), 1)

    def columns(ref):
        table = ref[...].astype(jnp.float32)
        return [
            jnp.sum(jnp.where(eye, table[k : k + 1], 0.0), axis=1, keepdims=True).astype(jnp.int32)
            for k in range(8)
        ]

    cand_load.wait()
    cand = columns(cand_ref)
    low = jnp.full((16, 128), 65536.0, jnp.float32)
    high = jnp.full((16, 128), -1.0, jnp.float32)
    for k in range(8):
        c = cand[k]
        key = ((row * 8 + k) * 256 + (c & 255)).astype(jnp.float32)
        hit = (c >> 8) == lane
        low = jnp.minimum(low, jnp.where(hit, key, 65536.0))
        high = jnp.maximum(high, jnp.where(hit, key, -1.0))
    low = jnp.min(low, axis=0, keepdims=True)
    high = jnp.max(high, axis=0, keepdims=True)
    used = high >= 0.0
    low_i = jnp.where(used, low, 0.0).astype(jnp.int32)
    high_i = jnp.where(used, high, 0.0).astype(jnp.int32)
    sel_v[...] = (low_i >> 11) + (high_i >> 11) * 16
    key = (low_i & 255) + (high_i & 255) * 256
    key_v[...] = key
    k_all[0] = key
    first_flat = low_i >> 8

    sel_copy = pltpu.make_async_copy(sel_v, sel_s, loc_sem)
    sel_copy.start()
    sel_copy.wait()

    qt_load.wait()
    v = sel_s[0, me]
    recv[0, 0] = qt_ref[v & 15]
    recv[0, 1] = qt_ref[(v >> 4) & 15]

    @pl.loop(1, N_DEV)
    def _(j):
        dg, ds = ahead(j)
        v = sel_s[0, dg * N_SHARD + ds]
        stage[j, 0] = qt_ref[v & 15]
        stage[j, 1] = qt_ref[(v >> 4) & 15]

    qp_load.wait()
    all_qp[s] = qp_ref[...]

    pl.semaphore_wait(barrier, N_SHARD + N_GROUP - 2)

    @pl.loop(1, N_GROUP)
    def _(i):
        pl.semaphore_signal(
            ready_sem, inc=1, device_id=((g + i) % N_GROUP, s), device_id_type=MESH
        )

    def send_key(j):
        pltpu.make_async_remote_copy(
            key_v, k_all.at[j], k_send, k_recv.at[lax.div(j, BATCH)], ahead(j), MESH
        ).start()

    def send_tokens(j):
        pltpu.make_async_remote_copy(
            stage.at[j], recv.at[j], send_sem, recv_sem.at[lax.div(j, HALF)], ahead(j), MESH
        ).start()

    def mates(send):
        @pl.loop(1, N_SHARD)
        def _(i):
            send(place(0, 0, lax.div(i, 4), mod4(i)))

        @pl.loop(1, N_GROUP)
        def _(i):
            send(place(lax.div(i, 2), lax.rem(i, 2), 0, 0))

    def other(send):
        def guarded(j):
            dy, dc, dz, dx = offsets(j)

            @pl.when(jnp.logical_and(dy + dc > 0, dz + dx > 0))
            def _():
                send(j)

        return guarded

    mates(send_key)

    @pl.loop(1, N_SHARD)
    def _(i):
        pltpu.make_async_remote_copy(
            qp_ref, all_qp.at[s], qp_send, qp_recv, (g, lax.rem(s + i, N_SHARD)), MESH
        ).start()

    mates(send_tokens)
    pl.semaphore_wait(ready_sem, N_GROUP - 1)
    pl.loop(1, LEAD)(other(send_key))

    @pl.loop(LEAD, N_DEV)
    def _(j):
        other(send_key)(j)
        other(send_tokens)(j - LEAD)

    pl.loop(N_DEV - LEAD, N_DEV)(other(send_tokens))

    def key_rows(b):
        rows = pl.ds(b * BATCH, BATCH)
        return pltpu.make_async_copy(k_all.at[rows], k_smem.at[rows], k_sem.at[b])

    pltpu.make_async_copy(k_all.at[pl.ds(1, BATCH - 1)], k_all.at[pl.ds(1, BATCH - 1)], k_recv.at[0]).wait()
    key_rows(0).start()

    pp_load.wait()

    pltpu.make_async_copy(all_qp.at[pl.ds(0, 15)], all_qp.at[pl.ds(0, 15)], qp_recv).wait()
    scores = lax.dot_general(
        all_qp[...].reshape(256, 256), pp_ref[...], (((1,), (1,)), ((), ())),
        preferred_element_type=jnp.float32,
    )
    lane2 = lax.broadcasted_iota(jnp.int32, (256, 128), 1)
    best = jnp.zeros((256, 128), jnp.float32)
    for c in range(4):
        half = scores[:, 128 * (c // 2) : 128 * (c // 2) + 128]
        top = jnp.max(jnp.where(lane2 // CSIZE == c % 2, half, -jnp.inf), axis=1, keepdims=True)
        best = jnp.where(lane2 == 4 * s + c, top, best)
    c_stage[...] = best.reshape(16, 16, 128)
    c_recv[s] = c_stage[s]

    @pl.loop(1, N_SHARD)
    def _(i):
        mate = (s + i) % N_SHARD
        pltpu.make_async_remote_copy(
            c_stage.at[mate], c_recv.at[s], c_send, c_rsem, (g, mate), MESH
        ).start()

    pt_load.wait()

    lane_r = lax.broadcasted_iota(jnp.int32, (2, 128), 1)
    own = lax.broadcasted_iota(jnp.int32, (2, 64), 1) // 32 == lax.broadcasted_iota(
        jnp.int32, (2, 64), 0
    )
    none = jnp.zeros((32, 128), jnp.bfloat16)

    def score(j):
        w = k_smem[j, 0, me]
        texts = jnp.concatenate([pt[w & 255], pt[(w >> 8) & 255]], axis=1)
        tokens = jnp.concatenate(
            [
                jnp.concatenate([recv[j, 0], none], axis=1),
                jnp.concatenate([none, recv[j, 1]], axis=1),
            ],
            axis=0,
        )
        sim = lax.dot_general(
            texts, tokens, (((1,), (1,)), ((), ())), preferred_element_type=jnp.float32
        )
        top = jnp.max(sim, axis=0, keepdims=True)
        mean = jnp.sum(jnp.where(own, top, 0.0), axis=1, keepdims=True) * (1.0 / 32)
        return jnp.where(lane_r == me, mean, 0.0)

    def back(j):
        pltpu.make_async_remote_copy(
            r_stage.at[j], r_recv.at[j], r_send, r_rsem, behind(j), MESH
        ).start()

    def arrived(first, count, h):
        rows = recv.at[pl.ds(first, count)]
        pltpu.make_async_copy(rows, rows, recv_sem.at[h]).wait()

    def batch(first, count):
        for t in range(count):
            r_stage[first + t] = score(first + t)

    def next_keys(b):
        rows = k_all.at[pl.ds(b * BATCH, BATCH)]
        pltpu.make_async_copy(rows, rows, k_recv.at[b]).wait()
        key_rows(b).start()

    key_rows(0).wait()
    arrived(1, HALF - 1, 0)
    next_keys(1)
    batch(0, HALF)
    arrived(HALF, HALF, 1)
    batch(HALF, HALF)
    r_recv[0] = r_stage[0]
    pl.loop(1, BATCH)(back)

    @pl.loop(1, N_BATCH - 1)
    def _(b):
        first = b * BATCH
        arrived(first, HALF, 2 * b)
        arrived(first + HALF, HALF, 2 * b + 1)
        next_keys(b + 1)
        key_rows(b).wait()
        batch(first, BATCH)
        for t in range(BATCH):
            back(first + t)

    key_rows(N_BATCH - 1).wait()

    @pl.loop(2 * N_BATCH - 2, 2 * N_BATCH)
    def _(h):
        arrived(h * HALF, HALF, h)
        batch(h * HALF, HALF)
        for t in range(HALF):
            back(h * HALF + t)

    lane8 = lax.broadcasted_iota(jnp.int32, (16, 8), 1)

    pltpu.make_async_copy(c_recv.at[pl.ds(0, 15)], c_recv.at[pl.ds(0, 15)], c_rsem).wait()
    probes_load.wait()
    all_best = jnp.sum(c_recv[...], axis=0)
    probes = columns(probes_ref)
    out = jnp.zeros((16, 8), jnp.float32)
    for k in range(8):
        pick = jnp.sum(jnp.where(probes[k] == lane, all_best, 0.0), axis=1, keepdims=True)
        out = jnp.where(lane8 == k, pick, out)
    coarse_ref[...] = out

    pltpu.make_async_copy(r_recv.at[pl.ds(1, 127)], r_recv.at[pl.ds(1, 127)], r_rsem).wait()
    both = jnp.sum(r_recv[...], axis=0)
    out = jnp.zeros((16, 8), jnp.float32)
    for k in range(8):
        here = (cand[k] >> 8) == lane
        value = jnp.where(first_flat == row * 8 + k, both[0:1], both[1:2])
        pick = jnp.sum(jnp.where(here, value, 0.0), axis=1, keepdims=True)
        out = jnp.where(lane8 == k, pick, out)
    rerank_ref[...] = out

    def sent(ref, sem):
        pltpu.make_async_copy(ref, ref, sem).wait()

    sent(stage.at[pl.ds(1, 127)], send_sem)
    sent(all_qp.at[pl.ds(0, 15)], qp_send)
    sent(k_all.at[pl.ds(1, 127)], k_send)
    sent(c_recv.at[pl.ds(0, 15)], c_send)
    sent(r_stage.at[pl.ds(1, 127)], r_send)


def body(query_prefix, query_tokens, probes, candidates, passage_prefix, passage_tokens):
    vmem = pl.BlockSpec(memory_space=pltpu.VMEM)
    dma = pltpu.SemaphoreType.DMA
    return tuple(
        pl.pallas_call(
            kernel,
            out_shape=(
                jax.ShapeDtypeStruct((16, 8), jnp.float32),
                jax.ShapeDtypeStruct((16, 8), jnp.float32),
            ),
            in_specs=[pl.BlockSpec(memory_space=pltpu.HBM)] * 6,
            out_specs=(vmem, vmem),
            scratch_shapes=[
                pltpu.VMEM((16, 256), jnp.bfloat16),
                pltpu.VMEM((16, 32, 128), jnp.bfloat16),
                pltpu.VMEM((8, 16), jnp.int32),
                pltpu.VMEM((8, 16), jnp.int32),
                pltpu.VMEM((256, 256), jnp.bfloat16),
                pltpu.VMEM((256, 128, 128), jnp.bfloat16),
                pltpu.VMEM((N_DEV, 2, 32, 128), jnp.bfloat16),
                pltpu.VMEM((N_DEV, 2, 32, 128), jnp.bfloat16),
                pltpu.VMEM((16, 16, 256), jnp.bfloat16),
                pltpu.VMEM((16, 16, 128), jnp.float32),
                pltpu.VMEM((16, 16, 128), jnp.float32),
                pltpu.VMEM((1, 128), jnp.int32),
                pltpu.VMEM((1, 128), jnp.int32),
                pltpu.VMEM((N_DEV, 1, 128), jnp.int32),
                pltpu.VMEM((N_DEV, 2, 128), jnp.float32),
                pltpu.VMEM((N_DEV, 2, 128), jnp.float32),
                pltpu.SMEM((1, 128), jnp.int32),
                pltpu.SMEM((N_DEV, 1, 128), jnp.int32),
                dma((6,)), dma, dma((N_BATCH,)), pltpu.SemaphoreType.REGULAR,
                dma, dma((2 * N_BATCH,)), dma, dma, dma, dma((N_BATCH,)), dma, dma, dma, dma,
            ],
            compiler_params=pltpu.CompilerParams(
                collective_id=0, has_side_effects=True, vmem_limit_bytes=60 * 1024 * 1024
            ),
            cost_estimate=pl.CostEstimate(
                flops=300_000_000, bytes_accessed=8_700_000, transcendentals=0
            ),
        )(query_prefix, query_tokens, probes.T, candidates.T, passage_prefix, passage_tokens)
    )


def solution(mesh):
    both = ("group", "shard")
    flat, cube = P(both, None), P(both, None, None)
    return jax.shard_map(
        body,
        mesh=mesh,
        in_specs=(flat, cube, flat, flat, flat, cube),
        out_specs=(flat, flat),
        check_vma=False,
    )
```

```python
import functools

import jax
import jax.numpy as jnp
from jax import lax
from jax.experimental import pallas as pl
from jax.experimental.pallas import tpu as pltpu
from jax.sharding import PartitionSpec as P

CSIZE = 64
N_DEV = 128
N_GROUP = 8
N_SHARD = 16
BATCH = 16
HALF = BATCH // 2
LEAD = 16
N_BATCH = N_DEV // BATCH
MESH = pl.DeviceIdType.MESH


def relative_places():
    steps = [
        (dy, dc, dz, dx) for dy in range(4) for dc in range(2) for dz in range(4) for dx in range(4)
    ]
    near = [0, 1, 2, 1]
    shuffled = [steps[37 * i % N_DEV] for i in range(N_DEV)]
    shuffled.sort(key=lambda o: -(near[o[0]] + near[o[2]] + near[o[3]]))
    is_mate = lambda o: o[0] + o[1] == 0 or o[2] + o[3] == 0
    mates = [o for o in shuffled if is_mate(o) and any(o)]
    return [(0, 0, 0, 0)] + mates + [o for o in shuffled if not is_mate(o)]


PLACES = relative_places()
N_MATES = N_GROUP + N_SHARD - 1


def kernel(
    qp_hbm, qt_hbm, probes_hbm, cand_hbm, pp_hbm, pt_hbm,
    out_ref,
    qp_ref, qt_ref, probes_ref, cand_ref, pp_ref, pt, stage, recv, all_qp, c_stage, c_recv, sel_v, key_v, k_all, r_stage, r_recv,
    sel_s, k_smem,
    in_sem, loc_sem, k_sem, ready_sem, send_sem, recv_sem, qp_send, qp_recv, k_send, k_recv,
    c_send, c_rsem, r_send, r_rsem,
):
    g = lax.axis_index("group")
    s = lax.axis_index("shard")
    me = g * N_SHARD + s
    y, core, z, x = g // 2, g % 2, s // 4, s % 4

    ys = [lax.rem(y + k, 4) * 2 for k in range(4)]
    cores = [core, 1 - core]
    zs = [lax.rem(z + k, 4) * 4 for k in range(4)]
    xs = [lax.rem(x + k, 4) for k in range(4)]

    def ahead(j):
        dy, dc, dz, dx = PLACES[j]
        return ys[dy] + cores[dc], zs[dz] + xs[dx]

    def behind(j):
        dy, dc, dz, dx = PLACES[j]
        return ys[-dy % 4] + cores[dc], zs[-dz % 4] + xs[-dx % 4]

    barrier = pltpu.get_barrier_semaphore()

    @pl.loop(1, N_SHARD)
    def _(i):
        pl.semaphore_signal(
            barrier, inc=1, device_id=(g, (s + i) % N_SHARD), device_id_type=MESH
        )

    @pl.loop(1, N_GROUP)
    def _(i):
        pl.semaphore_signal(
            barrier, inc=1, device_id=((g + i) % N_GROUP, s), device_id_type=MESH
        )

    loads = [
        pltpu.make_async_copy(src, dst, in_sem.at[i])
        for i, (src, dst) in enumerate(
            [(cand_hbm, cand_ref), (qt_hbm, qt_ref), (qp_hbm, qp_ref), (probes_hbm, probes_ref),
             (pp_hbm, pp_ref), (pt_hbm, pt)]
        )
    ]
    for load in loads:
        load.start()
    cand_load, qt_load, qp_load, probes_load, pp_load, pt_load = loads

    lane = lax.broadcasted_iota(jnp.int32, (16, 128), 1)
    row = lax.broadcasted_iota(jnp.int32, (16, 128), 0)
    eye = lax.broadcasted_iota(jnp.int32, (16, 16), 0) == lax.broadcasted_iota(jnp.int32, (16, 16), 1)

    def columns(ref):
        table = ref[...].astype(jnp.float32)
        return [
            jnp.sum(jnp.where(eye, table[k : k + 1], 0.0), axis=1, keepdims=True).astype(jnp.int32)
            for k in range(8)
        ]

    cand_load.wait()
    cand = columns(cand_ref)
    low = jnp.full((16, 128), 65536.0, jnp.float32)
    high = jnp.full((16, 128), -1.0, jnp.float32)
    for k in range(8):
        c = cand[k]
        key = ((row * 8 + k) * 256 + (c & 255)).astype(jnp.float32)
        hit = (c >> 8) == lane
        low = jnp.minimum(low, jnp.where(hit, key, 65536.0))
        high = jnp.maximum(high, jnp.where(hit, key, -1.0))
    low = jnp.min(low, axis=0, keepdims=True)
    high = jnp.max(high, axis=0, keepdims=True)
    used = high >= 0.0
    low_i = jnp.where(used, low, 0.0).astype(jnp.int32)
    high_i = jnp.where(used, high, 0.0).astype(jnp.int32)
    sel_v[...] = (low_i >> 11) + (high_i >> 11) * 16
    key = (low_i & 255) + (high_i & 255) * 256
    key_v[...] = key
    k_all[0] = key
    first_flat = low_i >> 8

    sel_copy = pltpu.make_async_copy(sel_v, sel_s, loc_sem)
    sel_copy.start()
    sel_copy.wait()

    qt_load.wait()
    v = sel_s[0, me]
    recv[0, 0] = qt_ref[v & 15]
    recv[0, 1] = qt_ref[(v >> 4) & 15]

    def fill(j):
        dg, ds = ahead(j)
        v = sel_s[0, dg * N_SHARD + ds]
        stage[j, 0] = qt_ref[v & 15]
        stage[j, 1] = qt_ref[(v >> 4) & 15]

    for j in range(1, N_MATES):
        fill(j)

    qp_load.wait()
    all_qp[s] = qp_ref[...]

    pl.semaphore_wait(barrier, N_SHARD + N_GROUP - 2)

    @pl.loop(1, N_GROUP)
    def _(i):
        pl.semaphore_signal(
            ready_sem, inc=1, device_id=((g + i) % N_GROUP, s), device_id_type=MESH
        )

    def send_key(j):
        pltpu.make_async_remote_copy(
            key_v, k_all.at[j], k_send, k_recv.at[j // BATCH], ahead(j), MESH
        ).start()

    def send_tokens(j):
        pltpu.make_async_remote_copy(
            stage.at[j], recv.at[j], send_sem, recv_sem.at[j // HALF], ahead(j), MESH
        ).start()

    for j in range(1, N_MATES):
        send_key(j)

    @pl.loop(1, N_SHARD)
    def _(i):
        pltpu.make_async_remote_copy(
            qp_ref, all_qp.at[s], qp_send, qp_recv, (g, lax.rem(s + i, N_SHARD)), MESH
        ).start()

    for j in range(1, N_MATES):
        send_tokens(j)
    for j in range(N_MATES, N_DEV):
        fill(j)
    pl.semaphore_wait(ready_sem, N_GROUP - 1)
    for j in range(N_MATES, N_DEV + LEAD):
        if j < N_DEV:
            send_key(j)
        if j >= N_MATES + LEAD:
            send_tokens(j - LEAD)

    def key_rows(b):
        rows = pl.ds(b * BATCH, BATCH)
        return pltpu.make_async_copy(k_all.at[rows], k_smem.at[rows], k_sem.at[b])

    pltpu.make_async_copy(k_all.at[pl.ds(1, BATCH - 1)], k_all.at[pl.ds(1, BATCH - 1)], k_recv.at[0]).wait()
    key_rows(0).start()

    pp_load.wait()

    pltpu.make_async_copy(all_qp.at[pl.ds(0, 15)], all_qp.at[pl.ds(0, 15)], qp_recv).wait()
    scores = lax.dot_general(
        all_qp[...].reshape(256, 256), pp_ref[...], (((1,), (1,)), ((), ())),
        preferred_element_type=jnp.float32,
    )
    lane2 = lax.broadcasted_iota(jnp.int32, (256, 128), 1)
    best = jnp.zeros((256, 128), jnp.float32)
    for c in range(4):
        half = scores[:, 128 * (c // 2) : 128 * (c // 2) + 128]
        top = jnp.max(jnp.where(lane2 // CSIZE == c % 2, half, -jnp.inf), axis=1, keepdims=True)
        best = jnp.where(lane2 == 4 * s + c, top, best)
    c_stage[...] = best.reshape(16, 16, 128)
    c_recv[s] = c_stage[s]

    @pl.loop(1, N_SHARD)
    def _(i):
        mate = (s + i) % N_SHARD
        pltpu.make_async_remote_copy(
            c_stage.at[mate], c_recv.at[s], c_send, c_rsem, (g, mate), MESH
        ).start()

    pt_load.wait()

    lane_r = lax.broadcasted_iota(jnp.int32, (2, 128), 1)
    own = lax.broadcasted_iota(jnp.int32, (2, 64), 1) // 32 == lax.broadcasted_iota(
        jnp.int32, (2, 64), 0
    )
    none = jnp.zeros((32, 128), jnp.bfloat16)

    def score(j):
        w = k_smem[j, 0, me]
        texts = jnp.concatenate([pt[w & 255], pt[(w >> 8) & 255]], axis=1)
        tokens = jnp.concatenate(
            [
                jnp.concatenate([recv[j, 0], none], axis=1),
                jnp.concatenate([none, recv[j, 1]], axis=1),
            ],
            axis=0,
        )
        sim = lax.dot_general(
            texts, tokens, (((1,), (1,)), ((), ())), preferred_element_type=jnp.float32
        )
        top = jnp.max(sim, axis=0, keepdims=True)
        mean = jnp.sum(jnp.where(own, top, 0.0), axis=1, keepdims=True) * (1.0 / 32)
        return jnp.where(lane_r == me, mean, 0.0)

    def back(j):
        pltpu.make_async_remote_copy(
            r_stage.at[j], r_recv.at[j], r_send, r_rsem, behind(j), MESH
        ).start()

    def arrived(first, count, h):
        rows = recv.at[pl.ds(first, count)]
        pltpu.make_async_copy(rows, rows, recv_sem.at[h]).wait()

    def batch(first, count):
        for t in range(count):
            r_stage[first + t] = score(first + t)

    def next_keys(b):
        rows = k_all.at[pl.ds(b * BATCH, BATCH)]
        pltpu.make_async_copy(rows, rows, k_recv.at[b]).wait()
        key_rows(b).start()

    key_rows(0).wait()
    arrived(1, HALF - 1, 0)
    next_keys(1)
    batch(0, HALF)
    arrived(HALF, HALF, 1)
    batch(HALF, HALF)
    r_recv[0] = r_stage[0]
    for j in range(1, BATCH):
        back(j)

    @pl.loop(1, N_BATCH - 1)
    def _(b):
        first = b * BATCH
        arrived(first, HALF, 2 * b)
        arrived(first + HALF, HALF, 2 * b + 1)
        next_keys(b + 1)
        key_rows(b).wait()
        batch(first, BATCH)
        for n in range(1, N_BATCH - 1):

            @pl.when(b == n)
            def _():
                for j in range(n * BATCH, (n + 1) * BATCH):
                    back(j)

    key_rows(N_BATCH - 1).wait()

    @pl.loop(2 * N_BATCH - 2, 2 * N_BATCH)
    def _(h):
        arrived(h * HALF, HALF, h)
        batch(h * HALF, HALF)
        for n in (2 * N_BATCH - 2, 2 * N_BATCH - 1):

            @pl.when(h == n)
            def _():
                for j in range(n * HALF, (n + 1) * HALF):
                    back(j)

    row8 = lax.broadcasted_iota(jnp.int32, (8, 16), 0)

    def across(column):
        return jnp.sum(jnp.where(eye, column, 0.0), axis=0, keepdims=True)


    pltpu.make_async_copy(c_recv.at[pl.ds(0, 15)], c_recv.at[pl.ds(0, 15)], c_rsem).wait()
    probes_load.wait()
    all_best = jnp.sum(c_recv[...], axis=0)
    probes = columns(probes_ref)
    out = jnp.zeros((8, 16), jnp.float32)
    for k in range(8):
        pick = jnp.sum(jnp.where(probes[k] == lane, all_best, 0.0), axis=1, keepdims=True)
        out = jnp.where(row8 == k, across(pick), out)
    out_ref[0] = out

    pltpu.make_async_copy(r_recv.at[pl.ds(1, 127)], r_recv.at[pl.ds(1, 127)], r_rsem).wait()
    both = jnp.sum(r_recv[...], axis=0)
    out = jnp.zeros((8, 16), jnp.float32)
    for k in range(8):
        here = (cand[k] >> 8) == lane
        value = jnp.where(first_flat == row * 8 + k, both[0:1], both[1:2])
        pick = jnp.sum(jnp.where(here, value, 0.0), axis=1, keepdims=True)
        out = jnp.where(row8 == k, across(pick), out)
    out_ref[1] = out

    def sent(ref, sem):
        pltpu.make_async_copy(ref, ref, sem).wait()

    sent(stage.at[pl.ds(1, 127)], send_sem)
    sent(all_qp.at[pl.ds(0, 15)], qp_send)
    sent(k_all.at[pl.ds(1, 127)], k_send)
    sent(c_recv.at[pl.ds(0, 15)], c_send)
    sent(r_stage.at[pl.ds(1, 127)], r_send)


def body(query_prefix, query_tokens, probes, candidates, passage_prefix, passage_tokens):
    vmem = pl.BlockSpec(memory_space=pltpu.VMEM)
    dma = pltpu.SemaphoreType.DMA
    scores = (
        pl.pallas_call(
            kernel,
            out_shape=jax.ShapeDtypeStruct((2, 8, 16), jnp.float32),
            in_specs=[pl.BlockSpec(memory_space=pltpu.HBM)] * 6,
            out_specs=vmem,
            scratch_shapes=[
                pltpu.VMEM((16, 256), jnp.bfloat16),
                pltpu.VMEM((16, 32, 128), jnp.bfloat16),
                pltpu.VMEM((8, 16), jnp.int32),
                pltpu.VMEM((8, 16), jnp.int32),
                pltpu.VMEM((256, 256), jnp.bfloat16),
                pltpu.VMEM((256, 128, 128), jnp.bfloat16),
                pltpu.VMEM((N_DEV, 2, 32, 128), jnp.bfloat16),
                pltpu.VMEM((N_DEV, 2, 32, 128), jnp.bfloat16),
                pltpu.VMEM((16, 16, 256), jnp.bfloat16),
                pltpu.VMEM((16, 16, 128), jnp.float32),
                pltpu.VMEM((16, 16, 128), jnp.float32),
                pltpu.VMEM((1, 128), jnp.int32),
                pltpu.VMEM((1, 128), jnp.int32),
                pltpu.VMEM((N_DEV, 1, 128), jnp.int32),
                pltpu.VMEM((N_DEV, 2, 128), jnp.float32),
                pltpu.VMEM((N_DEV, 2, 128), jnp.float32),
                pltpu.SMEM((1, 128), jnp.int32),
                pltpu.SMEM((N_DEV, 1, 128), jnp.int32),
                dma((6,)), dma, dma((N_BATCH,)), pltpu.SemaphoreType.REGULAR,
                dma, dma((2 * N_BATCH,)), dma, dma, dma, dma((N_BATCH,)), dma, dma, dma, dma,
            ],
            compiler_params=pltpu.CompilerParams(
                collective_id=0, has_side_effects=True, vmem_limit_bytes=60 * 1024 * 1024
            ),
            cost_estimate=pl.CostEstimate(
                flops=300_000_000, bytes_accessed=8_700_000, transcendentals=0
            ),
        )(query_prefix, query_tokens, probes.T, candidates.T, passage_prefix, passage_tokens)
    )
    return scores[0].T, scores[1].T


def solution(mesh):
    both = ("group", "shard")
    flat, cube = P(both, None), P(both, None, None)
    return jax.shard_map(
        body,
        mesh=mesh,
        in_specs=(flat, cube, flat, flat, flat, cube),
        out_specs=(flat, flat),
        check_vma=False,
    )
```

```python
import functools

import jax
import jax.numpy as jnp
from jax import lax
from jax.experimental import pallas as pl
from jax.experimental.pallas import tpu as pltpu
from jax.sharding import PartitionSpec as P

CSIZE = 64
N_DEV = 128
N_GROUP = 8
N_SHARD = 16
BATCH = 16
HALF = BATCH // 2
LEAD = 16
N_BATCH = N_DEV // BATCH
MESH = pl.DeviceIdType.MESH


def relative_places():
    steps = [
        (dy, dc, dz, dx) for dy in range(4) for dc in range(2) for dz in range(4) for dx in range(4)
    ]
    near = [0, 1, 2, 1]
    shuffled = [steps[37 * i % N_DEV] for i in range(N_DEV)]
    shuffled.sort(key=lambda o: -(near[o[0]] + near[o[2]] + near[o[3]]))
    is_mate = lambda o: o[0] + o[1] == 0 or o[2] + o[3] == 0
    mates = [o for o in shuffled if is_mate(o) and any(o)]
    return [(0, 0, 0, 0)] + mates + [o for o in shuffled if not is_mate(o)]


PLACES = relative_places()
SHARD_MATES = [j for j, o in enumerate(PLACES) if any(o) and o[0] + o[1] == 0]
GROUP_MATES = [j for j, o in enumerate(PLACES) if any(o) and o[2] + o[3] == 0]
N_MATES = N_GROUP + N_SHARD - 1


def kernel(
    qp_hbm, qt_hbm, probes_hbm, cand_hbm, pp_hbm, pt_hbm,
    out_ref,
    qp_ref, qt_ref, probes_ref, cand_ref, pp_ref, pt, stage, recv, all_qp, c_stage, c_recv, sel_v, key_v, k_all, r_stage, r_recv,
    sel_s, k_smem,
    in_sem, loc_sem, k_sem, ready_sem, send_sem, recv_sem, qp_send, qp_recv, k_send, k_recv,
    c_send, c_rsem, r_send, r_rsem,
):
    g = lax.axis_index("group")
    s = lax.axis_index("shard")
    me = g * N_SHARD + s
    y, core, z, x = g // 2, g % 2, s // 4, s % 4

    ys = [lax.rem(y + k, 4) * 2 for k in range(4)]
    cores = [core, 1 - core]
    zs = [lax.rem(z + k, 4) * 4 for k in range(4)]
    xs = [lax.rem(x + k, 4) for k in range(4)]

    def ahead(j):
        dy, dc, dz, dx = PLACES[j]
        return ys[dy] + cores[dc], zs[dz] + xs[dx]

    def behind(j):
        dy, dc, dz, dx = PLACES[j]
        return ys[-dy % 4] + cores[dc], zs[-dz % 4] + xs[-dx % 4]

    loads = [
        pltpu.make_async_copy(src, dst, in_sem.at[i])
        for i, (src, dst) in enumerate(
            [(cand_hbm, cand_ref), (qt_hbm, qt_ref), (qp_hbm, qp_ref), (probes_hbm, probes_ref),
             (pp_hbm, pp_ref), (pt_hbm, pt)]
        )
    ]
    for load in loads[:2]:
        load.start()

    barrier = pltpu.get_barrier_semaphore()
    for j in range(1, N_MATES):
        pl.semaphore_signal(barrier, inc=1, device_id=ahead(j), device_id_type=MESH)
    for load in loads[2:]:
        load.start()
    cand_load, qt_load, qp_load, probes_load, pp_load, pt_load = loads

    lane = lax.broadcasted_iota(jnp.int32, (16, 128), 1)
    row = lax.broadcasted_iota(jnp.int32, (16, 128), 0)
    eye = lax.broadcasted_iota(jnp.int32, (16, 16), 0) == lax.broadcasted_iota(jnp.int32, (16, 16), 1)

    def columns(ref):
        table = ref[...].astype(jnp.float32)
        return [
            jnp.sum(jnp.where(eye, table[k : k + 1], 0.0), axis=1, keepdims=True).astype(jnp.int32)
            for k in range(8)
        ]

    cand_load.wait()
    cand = columns(cand_ref)
    low = jnp.full((16, 128), 65536.0, jnp.float32)
    high = jnp.full((16, 128), -1.0, jnp.float32)
    for k in range(8):
        c = cand[k]
        key = ((row * 8 + k) * 256 + (c & 255)).astype(jnp.float32)
        hit = (c >> 8) == lane
        low = jnp.minimum(low, jnp.where(hit, key, 65536.0))
        high = jnp.maximum(high, jnp.where(hit, key, -1.0))
    low = jnp.min(low, axis=0, keepdims=True)
    high = jnp.max(high, axis=0, keepdims=True)
    used = high >= 0.0
    low_i = jnp.where(used, low, 0.0).astype(jnp.int32)
    high_i = jnp.where(used, high, 0.0).astype(jnp.int32)
    sel_v[...] = (low_i >> 11) + (high_i >> 11) * 16
    key = (low_i & 255) + (high_i & 255) * 256
    key_v[...] = key
    k_all[0] = key
    first_flat = low_i >> 8

    sel_copy = pltpu.make_async_copy(sel_v, sel_s, loc_sem)
    sel_copy.start()
    sel_copy.wait()

    qt_load.wait()
    v = sel_s[0, me]
    recv[0, 0] = qt_ref[v & 15]
    recv[0, 1] = qt_ref[(v >> 4) & 15]

    def fill(j):
        dg, ds = ahead(j)
        v = sel_s[0, dg * N_SHARD + ds]
        stage[j, 0] = qt_ref[v & 15]
        stage[j, 1] = qt_ref[(v >> 4) & 15]

    for j in range(1, N_MATES):
        fill(j)

    qp_load.wait()
    all_qp[s] = qp_ref[...]

    pl.semaphore_wait(barrier, N_MATES - 1)
    for j in GROUP_MATES:
        pl.semaphore_signal(ready_sem, inc=1, device_id=ahead(j), device_id_type=MESH)

    def send_key(j):
        pltpu.make_async_remote_copy(
            key_v, k_all.at[j], k_send, k_recv.at[j // BATCH], ahead(j), MESH
        ).start()

    def send_tokens(j):
        pltpu.make_async_remote_copy(
            stage.at[j], recv.at[j], send_sem, recv_sem.at[j // HALF], ahead(j), MESH
        ).start()

    for j in range(1, N_MATES):
        send_key(j)

    for j in SHARD_MATES:
        pltpu.make_async_remote_copy(
            qp_ref, all_qp.at[s], qp_send, qp_recv, ahead(j), MESH
        ).start()
    for j in range(1, N_MATES):
        send_tokens(j)
    for j in range(N_MATES, N_DEV):
        fill(j)
    pl.semaphore_wait(ready_sem, N_GROUP - 1)
    for j in range(N_MATES, N_DEV + LEAD):
        if j < N_DEV:
            send_key(j)
        if j >= N_MATES + LEAD:
            send_tokens(j - LEAD)

    def key_rows(b):
        rows = pl.ds(b * BATCH, BATCH)
        return pltpu.make_async_copy(k_all.at[rows], k_smem.at[rows], k_sem.at[b])

    pltpu.make_async_copy(k_all.at[pl.ds(1, BATCH - 1)], k_all.at[pl.ds(1, BATCH - 1)], k_recv.at[0]).wait()
    key_rows(0).start()

    pt_load.wait()

    lane_r = lax.broadcasted_iota(jnp.int32, (2, 128), 1)
    own = lax.broadcasted_iota(jnp.int32, (2, 64), 1) // 32 == lax.broadcasted_iota(
        jnp.int32, (2, 64), 0
    )
    none = jnp.zeros((32, 128), jnp.bfloat16)

    def score(j):
        w = k_smem[j, 0, me]
        texts = jnp.concatenate([pt[w & 255], pt[(w >> 8) & 255]], axis=1)
        tokens = jnp.concatenate(
            [
                jnp.concatenate([recv[j, 0], none], axis=1),
                jnp.concatenate([none, recv[j, 1]], axis=1),
            ],
            axis=0,
        )
        sim = lax.dot_general(
            texts, tokens, (((1,), (1,)), ((), ())), preferred_element_type=jnp.float32
        )
        top = jnp.max(sim, axis=0, keepdims=True)
        mean = jnp.sum(jnp.where(own, top, 0.0), axis=1, keepdims=True) * (1.0 / 32)
        return jnp.where(lane_r == me, mean, 0.0)

    def back(j):
        pltpu.make_async_remote_copy(
            r_stage.at[j], r_recv.at[j], r_send, r_rsem, behind(j), MESH
        ).start()

    def arrived(first, count, h):
        rows = recv.at[pl.ds(first, count)]
        pltpu.make_async_copy(rows, rows, recv_sem.at[h]).wait()

    def batch(first, count):
        for t in range(count):
            r_stage[first + t] = score(first + t)

    def next_keys(b):
        rows = k_all.at[pl.ds(b * BATCH, BATCH)]
        pltpu.make_async_copy(rows, rows, k_recv.at[b]).wait()
        key_rows(b).start()

    key_rows(0).wait()
    arrived(1, HALF - 1, 0)
    next_keys(1)
    batch(0, HALF)
    arrived(HALF, HALF, 1)
    batch(HALF, HALF)
    r_recv[0] = r_stage[0]
    for j in range(1, BATCH):
        back(j)

    pp_load.wait()

    pltpu.make_async_copy(all_qp.at[pl.ds(0, 15)], all_qp.at[pl.ds(0, 15)], qp_recv).wait()
    scores = lax.dot_general(
        pp_ref[...], all_qp[...].reshape(256, 256), (((1,), (1,)), ((), ())),
        preferred_element_type=jnp.float32,
    )
    best = jnp.concatenate(
        [jnp.max(scores[c * CSIZE : (c + 1) * CSIZE], axis=0, keepdims=True) for c in range(4)], axis=0
    )
    c_stage[0] = best[:, :128]
    c_stage[1] = best[:, 128:]
    c_recv[s] = c_stage[lax.div(s, 8)]
    for j in SHARD_MATES:
        to = ahead(j)
        pltpu.make_async_remote_copy(
            c_stage.at[lax.div(to[1], 8)], c_recv.at[s], c_send, c_rsem, to, MESH
        ).start()

    @pl.loop(1, N_BATCH - 1)
    def _(b):
        first = b * BATCH
        arrived(first, HALF, 2 * b)
        arrived(first + HALF, HALF, 2 * b + 1)
        next_keys(b + 1)
        key_rows(b).wait()
        batch(first, BATCH)
        for n in range(1, N_BATCH - 1):

            @pl.when(b == n)
            def _():
                for j in range(n * BATCH, (n + 1) * BATCH):
                    back(j)

    key_rows(N_BATCH - 1).wait()

    @pl.loop(2 * N_BATCH - 2, 2 * N_BATCH)
    def _(h):
        arrived(h * HALF, HALF, h)
        batch(h * HALF, HALF)
        for n in (2 * N_BATCH - 2, 2 * N_BATCH - 1):

            @pl.when(h == n)
            def _():
                for j in range(n * HALF, (n + 1) * HALF):
                    back(j)

    row8 = lax.broadcasted_iota(jnp.int32, (8, 16), 0)

    def across(column):
        return jnp.sum(jnp.where(eye, column, 0.0), axis=0, keepdims=True)


    pltpu.make_async_copy(c_recv.at[pl.ds(0, 15)], c_recv.at[pl.ds(0, 15)], c_rsem).wait()
    probes_load.wait()
    all_best = c_recv[...]
    cluster = 4 * lax.broadcasted_iota(jnp.int32, (16, 4, 128), 0) + lax.broadcasted_iota(
        jnp.int32, (16, 4, 128), 1
    )
    first_lane = lax.rem(s, 8) * 16
    probes = jnp.concatenate([probes_ref[...], jnp.zeros((8, 112), jnp.int32)], axis=1)
    probes = pltpu.roll(probes, first_lane, 1)
    row_k = lax.broadcasted_iota(jnp.int32, (8, 128), 0)
    out = jnp.zeros((8, 128), jnp.float32)
    for k in range(8):
        hit = probes[k : k + 1][None] == cluster
        pick = jnp.sum(jnp.sum(jnp.where(hit, all_best, 0.0), axis=0), axis=0, keepdims=True)
        out = jnp.where(row_k == k, pick, out)
    out = pltpu.roll(out, lax.rem(128 - first_lane, 128), 1)[:, :16]
    out_ref[0] = out

    pltpu.make_async_copy(r_recv.at[pl.ds(1, 127)], r_recv.at[pl.ds(1, 127)], r_rsem).wait()
    both = jnp.sum(r_recv[...], axis=0)
    out = jnp.zeros((8, 16), jnp.float32)
    for k in range(8):
        here = (cand[k] >> 8) == lane
        value = jnp.where(first_flat == row * 8 + k, both[0:1], both[1:2])
        pick = jnp.sum(jnp.where(here, value, 0.0), axis=1, keepdims=True)
        out = jnp.where(row8 == k, across(pick), out)
    out_ref[1] = out

    def sent(ref, sem):
        pltpu.make_async_copy(ref, ref, sem).wait()

    sent(stage.at[pl.ds(1, 127)], send_sem)
    sent(all_qp.at[pl.ds(0, 15)], qp_send)
    sent(k_all.at[pl.ds(1, 127)], k_send)
    sent(c_recv.at[pl.ds(0, 15)], c_send)
    sent(r_stage.at[pl.ds(1, 127)], r_send)


def body(query_prefix, query_tokens, probes, candidates, passage_prefix, passage_tokens):
    vmem = pl.BlockSpec(memory_space=pltpu.VMEM)
    dma = pltpu.SemaphoreType.DMA
    scores = (
        pl.pallas_call(
            kernel,
            out_shape=jax.ShapeDtypeStruct((2, 8, 16), jnp.float32),
            in_specs=[pl.BlockSpec(memory_space=pltpu.HBM)] * 6,
            out_specs=vmem,
            scratch_shapes=[
                pltpu.VMEM((16, 256), jnp.bfloat16),
                pltpu.VMEM((16, 32, 128), jnp.bfloat16),
                pltpu.VMEM((8, 16), jnp.int32),
                pltpu.VMEM((8, 16), jnp.int32),
                pltpu.VMEM((256, 256), jnp.bfloat16),
                pltpu.VMEM((256, 128, 128), jnp.bfloat16),
                pltpu.VMEM((N_DEV, 2, 32, 128), jnp.bfloat16),
                pltpu.VMEM((N_DEV, 2, 32, 128), jnp.bfloat16),
                pltpu.VMEM((16, 16, 256), jnp.bfloat16),
                pltpu.VMEM((2, 4, 128), jnp.float32),
                pltpu.VMEM((16, 4, 128), jnp.float32),
                pltpu.VMEM((1, 128), jnp.int32),
                pltpu.VMEM((1, 128), jnp.int32),
                pltpu.VMEM((N_DEV, 1, 128), jnp.int32),
                pltpu.VMEM((N_DEV, 2, 128), jnp.float32),
                pltpu.VMEM((N_DEV, 2, 128), jnp.float32),
                pltpu.SMEM((1, 128), jnp.int32),
                pltpu.SMEM((N_DEV, 1, 128), jnp.int32),
                dma((6,)), dma, dma((N_BATCH,)), pltpu.SemaphoreType.REGULAR,
                dma, dma((2 * N_BATCH,)), dma, dma, dma, dma((N_BATCH,)), dma, dma, dma, dma,
            ],
            compiler_params=pltpu.CompilerParams(
                collective_id=0, has_side_effects=True, vmem_limit_bytes=60 * 1024 * 1024
            ),
            cost_estimate=pl.CostEstimate(
                flops=300_000_000, bytes_accessed=8_700_000, transcendentals=0
            ),
        )(query_prefix, query_tokens, probes.T, candidates.T, passage_prefix, passage_tokens)
    )
    return scores[0].T, scores[1].T


def solution(mesh):
    both = ("group", "shard")
    flat, cube = P(both, None), P(both, None, None)
    return jax.shard_map(
        body,
        mesh=mesh,
        in_specs=(flat, cube, flat, flat, flat, cube),
        out_specs=(flat, flat),
        check_vma=False,
    )
```

```python
import functools

import jax
import jax.numpy as jnp
from jax import lax
from jax.experimental import pallas as pl
from jax.experimental.pallas import tpu as pltpu
from jax.sharding import PartitionSpec as P

CSIZE = 64
N_DEV = 128
N_GROUP = 8
N_SHARD = 16
BATCH = 16
HALF = BATCH // 2
LEAD = 16
N_BATCH = N_DEV // BATCH
MESH = pl.DeviceIdType.MESH


def relative_places():
    steps = [
        (dy, dc, dz, dx) for dy in range(4) for dc in range(2) for dz in range(4) for dx in range(4)
    ]
    near = [0, 1, 2, 1]
    shuffled = [steps[37 * i % N_DEV] for i in range(N_DEV)]
    shuffled.sort(key=lambda o: -(near[o[0]] + near[o[2]] + near[o[3]]))
    is_mate = lambda o: o[0] + o[1] == 0 or o[2] + o[3] == 0
    mates = [o for o in shuffled if is_mate(o) and any(o)]
    return [(0, 0, 0, 0)] + mates + [o for o in shuffled if not is_mate(o)]


PLACES = relative_places()
SHARD_MATES = [j for j, o in enumerate(PLACES) if any(o) and o[0] + o[1] == 0]
GROUP_MATES = [j for j, o in enumerate(PLACES) if any(o) and o[2] + o[3] == 0]
N_MATES = N_GROUP + N_SHARD - 1


def kernel(
    qp_hbm, qt_hbm, probes_hbm, cand_hbm, pp_hbm, pt_hbm,
    out_ref,
    qp_ref, qt_ref, probes_ref, cand_ref, pp_ref, pt, stage, recv, all_qp, c_stage, c_recv, sel_v, key_v, k_all, r_stage, r_recv,
    sel_s, k_smem,
    in_sem, loc_sem, k_sem, ready_sem, send_sem, recv_sem, qp_send, qp_recv, k_send, k_recv,
    c_send, c_rsem, r_send, r_rsem,
):
    g = lax.axis_index("group")
    s = lax.axis_index("shard")
    me = g * N_SHARD + s
    y, core, z, x = g // 2, g % 2, s // 4, s % 4

    ys = [lax.rem(y + k, 4) * 2 for k in range(4)]
    cores = [core, 1 - core]
    zs = [lax.rem(z + k, 4) * 4 for k in range(4)]
    xs = [lax.rem(x + k, 4) for k in range(4)]

    def ahead(j):
        dy, dc, dz, dx = PLACES[j]
        return ys[dy] + cores[dc], zs[dz] + xs[dx]

    def behind(j):
        dy, dc, dz, dx = PLACES[j]
        return ys[-dy % 4] + cores[dc], zs[-dz % 4] + xs[-dx % 4]

    loads = [
        pltpu.make_async_copy(src, dst, in_sem.at[i])
        for i, (src, dst) in enumerate(
            [(cand_hbm, cand_ref), (qt_hbm, qt_ref), (qp_hbm, qp_ref), (probes_hbm, probes_ref),
             (pp_hbm, pp_ref), (pt_hbm, pt)]
        )
    ]
    for load in loads[:2]:
        load.start()

    barrier = pltpu.get_barrier_semaphore()
    for j in range(1, N_MATES):
        pl.semaphore_signal(barrier, inc=1, device_id=ahead(j), device_id_type=MESH)
    for load in loads[2:]:
        load.start()
    cand_load, qt_load, qp_load, probes_load, pp_load, pt_load = loads

    lane = lax.broadcasted_iota(jnp.int32, (16, 128), 1)
    row = lax.broadcasted_iota(jnp.int32, (16, 128), 0)
    eye = lax.broadcasted_iota(jnp.int32, (16, 16), 0) == lax.broadcasted_iota(jnp.int32, (16, 16), 1)

    def columns(ref):
        table = ref[...].astype(jnp.float32)
        return [
            jnp.sum(jnp.where(eye, table[k : k + 1], 0.0), axis=1, keepdims=True).astype(jnp.int32)
            for k in range(8)
        ]

    cand_load.wait()
    cand = columns(cand_ref)
    low = jnp.full((16, 128), 65536.0, jnp.float32)
    high = jnp.full((16, 128), -1.0, jnp.float32)
    for k in range(8):
        c = cand[k]
        key = ((row * 8 + k) * 256 + (c & 255)).astype(jnp.float32)
        hit = (c >> 8) == lane
        low = jnp.minimum(low, jnp.where(hit, key, 65536.0))
        high = jnp.maximum(high, jnp.where(hit, key, -1.0))
    low = jnp.min(low, axis=0, keepdims=True)
    high = jnp.max(high, axis=0, keepdims=True)
    used = high >= 0.0
    low_i = jnp.where(used, low, 0.0).astype(jnp.int32)
    high_i = jnp.where(used, high, 0.0).astype(jnp.int32)
    sel_v[...] = (low_i >> 11) + (high_i >> 11) * 16
    key = (low_i & 255) + (high_i & 255) * 256
    key_v[...] = key
    k_all[0] = key
    first_flat = low_i >> 8

    sel_copy = pltpu.make_async_copy(sel_v, sel_s, loc_sem)
    sel_copy.start()
    sel_copy.wait()

    qt_load.wait()
    v = sel_s[0, me]
    recv[0, 0] = qt_ref[v & 15]
    recv[0, 1] = qt_ref[(v >> 4) & 15]

    def fill(j):
        dg, ds = ahead(j)
        v = sel_s[0, dg * N_SHARD + ds]
        stage[j, 0] = qt_ref[v & 15]
        stage[j, 1] = qt_ref[(v >> 4) & 15]

    for j in range(1, N_MATES):
        fill(j)

    qp_load.wait()
    all_qp[s] = qp_ref[...]

    pl.semaphore_wait(barrier, N_MATES - 1)
    for j in GROUP_MATES:
        pl.semaphore_signal(ready_sem, inc=1, device_id=ahead(j), device_id_type=MESH)

    def send_key(j):
        pltpu.make_async_remote_copy(
            key_v, k_all.at[j], k_send, k_recv.at[j // BATCH], ahead(j), MESH
        ).start()

    def send_tokens(j):
        pltpu.make_async_remote_copy(
            stage.at[j], recv.at[j], send_sem, recv_sem.at[j // HALF], ahead(j), MESH
        ).start()

    for j in range(1, N_MATES):
        send_key(j)

    for j in SHARD_MATES:
        pltpu.make_async_remote_copy(
            qp_ref, all_qp.at[s], qp_send, qp_recv, ahead(j), MESH
        ).start()
    for j in range(1, N_MATES):
        send_tokens(j)
    pl.semaphore_wait(ready_sem, N_GROUP - 1)
    for j in range(N_MATES, N_DEV + LEAD):
        if j < N_DEV:
            send_key(j)
        if j >= N_MATES + LEAD:
            fill(j - LEAD)
            send_tokens(j - LEAD)

    def key_rows(b):
        rows = pl.ds(b * BATCH, BATCH)
        return pltpu.make_async_copy(k_all.at[rows], k_smem.at[rows], k_sem.at[b])

    pltpu.make_async_copy(k_all.at[pl.ds(1, BATCH - 1)], k_all.at[pl.ds(1, BATCH - 1)], k_recv.at[0]).wait()
    key_rows(0).start()

    pt_load.wait()

    lane_r = lax.broadcasted_iota(jnp.int32, (2, 128), 1)
    own = lax.broadcasted_iota(jnp.int32, (2, 64), 1) // 32 == lax.broadcasted_iota(
        jnp.int32, (2, 64), 0
    )
    none = jnp.zeros((32, 128), jnp.bfloat16)

    def score(j):
        w = k_smem[j, 0, me]
        texts = jnp.concatenate([pt[w & 255], pt[(w >> 8) & 255]], axis=1)
        tokens = jnp.concatenate(
            [
                jnp.concatenate([recv[j, 0], none], axis=1),
                jnp.concatenate([none, recv[j, 1]], axis=1),
            ],
            axis=0,
        )
        sim = lax.dot_general(
            texts, tokens, (((1,), (1,)), ((), ())), preferred_element_type=jnp.float32
        )
        top = jnp.max(sim, axis=0, keepdims=True)
        mean = jnp.sum(jnp.where(own, top, 0.0), axis=1, keepdims=True) * (1.0 / 32)
        return jnp.where(lane_r == me, mean, 0.0)

    def back(j):
        pltpu.make_async_remote_copy(
            r_stage.at[j], r_recv.at[j], r_send, r_rsem, behind(j), MESH
        ).start()

    def arrived(first, count, h):
        rows = recv.at[pl.ds(first, count)]
        pltpu.make_async_copy(rows, rows, recv_sem.at[h]).wait()

    def batch(first, count):
        for t in range(count):
            r_stage[first + t] = score(first + t)

    def next_keys(b):
        rows = k_all.at[pl.ds(b * BATCH, BATCH)]
        pltpu.make_async_copy(rows, rows, k_recv.at[b]).wait()
        key_rows(b).start()

    key_rows(0).wait()
    arrived(1, HALF - 1, 0)
    next_keys(1)
    batch(0, HALF)
    arrived(HALF, HALF, 1)
    batch(HALF, HALF)
    r_recv[0] = r_stage[0]
    for j in range(1, BATCH):
        back(j)

    pp_load.wait()

    pltpu.make_async_copy(all_qp.at[pl.ds(0, 15)], all_qp.at[pl.ds(0, 15)], qp_recv).wait()
    scores = lax.dot_general(
        pp_ref[...], all_qp[...].reshape(256, 256), (((1,), (1,)), ((), ())),
        preferred_element_type=jnp.float32,
    )
    best = jnp.concatenate(
        [jnp.max(scores[c * CSIZE : (c + 1) * CSIZE], axis=0, keepdims=True) for c in range(4)], axis=0
    )
    c_stage[0] = best[:, :128]
    c_stage[1] = best[:, 128:]
    c_recv[s] = c_stage[lax.div(s, 8)]
    for j in SHARD_MATES:
        to = ahead(j)
        pltpu.make_async_remote_copy(
            c_stage.at[lax.div(to[1], 8)], c_recv.at[s], c_send, c_rsem, to, MESH
        ).start()

    @pl.loop(1, N_BATCH - 1)
    def _(b):
        first = b * BATCH
        arrived(first, HALF, 2 * b)
        arrived(first + HALF, HALF, 2 * b + 1)
        next_keys(b + 1)
        key_rows(b).wait()
        batch(first, BATCH)
        for n in range(1, N_BATCH - 1):

            @pl.when(b == n)
            def _():
                for j in range(n * BATCH, (n + 1) * BATCH):
                    back(j)

    key_rows(N_BATCH - 1).wait()

    @pl.loop(2 * N_BATCH - 2, 2 * N_BATCH)
    def _(h):
        arrived(h * HALF, HALF, h)
        batch(h * HALF, HALF)
        for n in (2 * N_BATCH - 2, 2 * N_BATCH - 1):

            @pl.when(h == n)
            def _():
                for j in range(n * HALF, (n + 1) * HALF):
                    back(j)

    row8 = lax.broadcasted_iota(jnp.int32, (8, 16), 0)

    def across(column):
        return jnp.sum(jnp.where(eye, column, 0.0), axis=0, keepdims=True)


    pltpu.make_async_copy(c_recv.at[pl.ds(0, 15)], c_recv.at[pl.ds(0, 15)], c_rsem).wait()
    probes_load.wait()
    all_best = c_recv[...]
    cluster = 4 * lax.broadcasted_iota(jnp.int32, (16, 4, 128), 0) + lax.broadcasted_iota(
        jnp.int32, (16, 4, 128), 1
    )
    first_lane = lax.rem(s, 8) * 16
    probes = jnp.concatenate([probes_ref[...], jnp.zeros((8, 112), jnp.int32)], axis=1)
    probes = pltpu.roll(probes, first_lane, 1)
    row_k = lax.broadcasted_iota(jnp.int32, (8, 128), 0)
    out = jnp.zeros((8, 128), jnp.float32)
    for k in range(8):
        hit = probes[k : k + 1][None] == cluster
        pick = jnp.sum(jnp.sum(jnp.where(hit, all_best, 0.0), axis=0), axis=0, keepdims=True)
        out = jnp.where(row_k == k, pick, out)
    out = pltpu.roll(out, lax.rem(128 - first_lane, 128), 1)[:, :16]
    out_ref[0] = out

    pltpu.make_async_copy(r_recv.at[pl.ds(1, 127)], r_recv.at[pl.ds(1, 127)], r_rsem).wait()
    both = jnp.sum(r_recv[...], axis=0)
    out = jnp.zeros((8, 16), jnp.float32)
    for k in range(8):
        here = (cand[k] >> 8) == lane
        value = jnp.where(first_flat == row * 8 + k, both[0:1], both[1:2])
        pick = jnp.sum(jnp.where(here, value, 0.0), axis=1, keepdims=True)
        out = jnp.where(row8 == k, across(pick), out)
    out_ref[1] = out

    def sent(ref, sem):
        pltpu.make_async_copy(ref, ref, sem).wait()

    sent(stage.at[pl.ds(1, 127)], send_sem)
    sent(all_qp.at[pl.ds(0, 15)], qp_send)
    sent(k_all.at[pl.ds(1, 127)], k_send)
    sent(c_recv.at[pl.ds(0, 15)], c_send)
    sent(r_stage.at[pl.ds(1, 127)], r_send)


def body(query_prefix, query_tokens, probes, candidates, passage_prefix, passage_tokens):
    vmem = pl.BlockSpec(memory_space=pltpu.VMEM)
    dma = pltpu.SemaphoreType.DMA
    scores = (
        pl.pallas_call(
            kernel,
            out_shape=jax.ShapeDtypeStruct((2, 8, 16), jnp.float32),
            in_specs=[pl.BlockSpec(memory_space=pltpu.HBM)] * 6,
            out_specs=vmem,
            scratch_shapes=[
                pltpu.VMEM((16, 256), jnp.bfloat16),
                pltpu.VMEM((16, 32, 128), jnp.bfloat16),
                pltpu.VMEM((8, 16), jnp.int32),
                pltpu.VMEM((8, 16), jnp.int32),
                pltpu.VMEM((256, 256), jnp.bfloat16),
                pltpu.VMEM((256, 128, 128), jnp.bfloat16),
                pltpu.VMEM((N_DEV, 2, 32, 128), jnp.bfloat16),
                pltpu.VMEM((N_DEV, 2, 32, 128), jnp.bfloat16),
                pltpu.VMEM((16, 16, 256), jnp.bfloat16),
                pltpu.VMEM((2, 4, 128), jnp.float32),
                pltpu.VMEM((16, 4, 128), jnp.float32),
                pltpu.VMEM((1, 128), jnp.int32),
                pltpu.VMEM((1, 128), jnp.int32),
                pltpu.VMEM((N_DEV, 1, 128), jnp.int32),
                pltpu.VMEM((N_DEV, 2, 128), jnp.float32),
                pltpu.VMEM((N_DEV, 2, 128), jnp.float32),
                pltpu.SMEM((1, 128), jnp.int32),
                pltpu.SMEM((N_DEV, 1, 128), jnp.int32),
                dma((6,)), dma, dma((N_BATCH,)), pltpu.SemaphoreType.REGULAR,
                dma, dma((2 * N_BATCH,)), dma, dma, dma, dma((N_BATCH,)), dma, dma, dma, dma,
            ],
            compiler_params=pltpu.CompilerParams(
                collective_id=0, has_side_effects=True, vmem_limit_bytes=60 * 1024 * 1024
            ),
            cost_estimate=pl.CostEstimate(
                flops=300_000_000, bytes_accessed=8_700_000, transcendentals=0
            ),
        )(query_prefix, query_tokens, probes.T, candidates.T, passage_prefix, passage_tokens)
    )
    return scores[0].T, scores[1].T


def solution(mesh):
    both = ("group", "shard")
    flat, cube = P(both, None), P(both, None, None)
    return jax.shard_map(
        body,
        mesh=mesh,
        in_specs=(flat, cube, flat, flat, flat, cube),
        out_specs=(flat, flat),
        check_vma=False,
    )
```

```python
import functools

import jax
import jax.numpy as jnp
from jax import lax
from jax.experimental import pallas as pl
from jax.experimental.pallas import tpu as pltpu
from jax.sharding import PartitionSpec as P

CSIZE = 64
N_DEV = 128
N_GROUP = 8
N_SHARD = 16
BATCH = 16
HALF = BATCH // 2
LEAD = 16
N_BATCH = N_DEV // BATCH
MESH = pl.DeviceIdType.MESH


def relative_places():
    steps = [
        (dy, dc, dz, dx) for dy in range(4) for dc in range(2) for dz in range(4) for dx in range(4)
    ]
    near = [0, 1, 2, 1]
    shuffled = [steps[37 * i % N_DEV] for i in range(N_DEV)]
    shuffled.sort(key=lambda o: -(near[o[0]] + near[o[2]] + near[o[3]]))
    is_mate = lambda o: o[0] + o[1] == 0 or o[2] + o[3] == 0
    mates = [o for o in shuffled if is_mate(o) and any(o)]
    return [(0, 0, 0, 0)] + mates + [o for o in shuffled if not is_mate(o)]


PLACES = relative_places()
SHARD_MATES = [j for j, o in enumerate(PLACES) if any(o) and o[0] + o[1] == 0]
GROUP_MATES = [j for j, o in enumerate(PLACES) if any(o) and o[2] + o[3] == 0]
N_MATES = N_GROUP + N_SHARD - 1


def kernel(
    qp_hbm, qt_hbm, probes_hbm, cand_hbm, pp_hbm, pt_hbm,
    out_ref,
    qp_ref, qt_ref, probes_ref, cand_ref, pp_ref, pt, stage, recv, all_qp, c_stage, c_recv, sel_v, key_v, k_all, r_stage, r_recv,
    sel_s, k_smem,
    in_sem, loc_sem, k_sem, ready_sem, send_sem, recv_sem, qp_send, qp_recv, k_send, k_recv,
    c_send, c_rsem, r_send, r_rsem,
):
    g = lax.axis_index("group")
    s = lax.axis_index("shard")
    me = g * N_SHARD + s
    y, core, z, x = g // 2, g % 2, s // 4, s % 4

    ys = [lax.rem(y + k, 4) * 2 for k in range(4)]
    cores = [core, 1 - core]
    zs = [lax.rem(z + k, 4) * 4 for k in range(4)]
    xs = [lax.rem(x + k, 4) for k in range(4)]

    def ahead(j):
        dy, dc, dz, dx = PLACES[j]
        return ys[dy] + cores[dc], zs[dz] + xs[dx]

    def behind(j):
        dy, dc, dz, dx = PLACES[j]
        return ys[-dy % 4] + cores[dc], zs[-dz % 4] + xs[-dx % 4]

    loads = [
        pltpu.make_async_copy(src, dst, in_sem.at[i])
        for i, (src, dst) in enumerate(
            [(cand_hbm, cand_ref), (qt_hbm, qt_ref), (qp_hbm, qp_ref), (probes_hbm, probes_ref),
             (pp_hbm, pp_ref), (pt_hbm, pt)]
        )
    ]
    for load in loads[:2]:
        load.start()

    barrier = pltpu.get_barrier_semaphore()
    for j in range(1, N_MATES):
        pl.semaphore_signal(barrier, inc=1, device_id=ahead(j), device_id_type=MESH)
    for load in loads[2:]:
        load.start()
    cand_load, qt_load, qp_load, probes_load, pp_load, pt_load = loads

    lane = lax.broadcasted_iota(jnp.int32, (16, 128), 1)
    row = lax.broadcasted_iota(jnp.int32, (16, 128), 0)
    eye = lax.broadcasted_iota(jnp.int32, (16, 16), 0) == lax.broadcasted_iota(jnp.int32, (16, 16), 1)

    def columns(ref):
        table = ref[...].astype(jnp.float32)
        return [
            jnp.sum(jnp.where(eye, table[k : k + 1], 0.0), axis=1, keepdims=True).astype(jnp.int32)
            for k in range(8)
        ]

    cand_load.wait()
    cand = columns(cand_ref)
    low = jnp.full((16, 128), 65536.0, jnp.float32)
    high = jnp.full((16, 128), -1.0, jnp.float32)
    for k in range(8):
        c = cand[k]
        key = ((row * 8 + k) * 256 + (c & 255)).astype(jnp.float32)
        hit = (c >> 8) == lane
        low = jnp.minimum(low, jnp.where(hit, key, 65536.0))
        high = jnp.maximum(high, jnp.where(hit, key, -1.0))
    low = jnp.min(low, axis=0, keepdims=True)
    high = jnp.max(high, axis=0, keepdims=True)
    used = high >= 0.0
    low_i = jnp.where(used, low, 0.0).astype(jnp.int32)
    high_i = jnp.where(used, high, 0.0).astype(jnp.int32)
    sel_v[...] = (low_i >> 11) + (high_i >> 11) * 16
    key = (low_i & 255) + (high_i & 255) * 256
    key_v[...] = key
    k_all[0] = key
    first_flat = low_i >> 8

    sel_copy = pltpu.make_async_copy(sel_v, sel_s, loc_sem)
    sel_copy.start()
    sel_copy.wait()

    qt_load.wait()
    v = sel_s[0, me]
    recv[0, 0] = qt_ref[v & 15]
    recv[0, 1] = qt_ref[(v >> 4) & 15]

    def fill(j):
        dg, ds = ahead(j)
        v = sel_s[0, dg * N_SHARD + ds]
        stage[j, 0] = qt_ref[v & 15]
        stage[j, 1] = qt_ref[(v >> 4) & 15]


    qp_load.wait()
    all_qp[s] = qp_ref[...]

    pl.semaphore_wait(barrier, N_MATES - 1)
    for j in GROUP_MATES:
        pl.semaphore_signal(ready_sem, inc=1, device_id=ahead(j), device_id_type=MESH)

    def send_key(j):
        pltpu.make_async_remote_copy(
            key_v, k_all.at[j], k_send, k_recv.at[j // BATCH], ahead(j), MESH
        ).start()

    def send_tokens(j):
        pltpu.make_async_remote_copy(
            stage.at[j], recv.at[j], send_sem, recv_sem.at[j // HALF], ahead(j), MESH
        ).start()

    for j in range(1, N_MATES):
        send_key(j)

    for j in SHARD_MATES:
        pltpu.make_async_remote_copy(
            qp_ref, all_qp.at[s], qp_send, qp_recv, ahead(j), MESH
        ).start()
    for j in range(1, N_MATES):
        fill(j)
        send_tokens(j)
    pl.semaphore_wait(ready_sem, N_GROUP - 1)
    for j in range(N_MATES, N_DEV + LEAD):
        if j < N_DEV:
            send_key(j)
        if j >= N_MATES + LEAD:
            fill(j - LEAD)
            send_tokens(j - LEAD)

    def key_rows(b):
        rows = pl.ds(b * BATCH, BATCH)
        return pltpu.make_async_copy(k_all.at[rows], k_smem.at[rows], k_sem.at[b])

    pltpu.make_async_copy(k_all.at[pl.ds(1, BATCH - 1)], k_all.at[pl.ds(1, BATCH - 1)], k_recv.at[0]).wait()
    key_rows(0).start()

    pt_load.wait()

    lane_r = lax.broadcasted_iota(jnp.int32, (2, 128), 1)
    own = lax.broadcasted_iota(jnp.int32, (2, 64), 1) // 32 == lax.broadcasted_iota(
        jnp.int32, (2, 64), 0
    )
    none = jnp.zeros((32, 128), jnp.bfloat16)

    def score(j):
        w = k_smem[j, 0, me]
        texts = jnp.concatenate([pt[w & 255], pt[(w >> 8) & 255]], axis=1)
        tokens = jnp.concatenate(
            [
                jnp.concatenate([recv[j, 0], none], axis=1),
                jnp.concatenate([none, recv[j, 1]], axis=1),
            ],
            axis=0,
        )
        sim = lax.dot_general(
            texts, tokens, (((1,), (1,)), ((), ())), preferred_element_type=jnp.float32
        )
        top = jnp.max(sim, axis=0, keepdims=True)
        mean = jnp.sum(jnp.where(own, top, 0.0), axis=1, keepdims=True) * (1.0 / 32)
        return jnp.where(lane_r == me, mean, 0.0)

    def back(j):
        pltpu.make_async_remote_copy(
            r_stage.at[j], r_recv.at[j], r_send, r_rsem, behind(j), MESH
        ).start()

    def arrived(first, count, h):
        rows = recv.at[pl.ds(first, count)]
        pltpu.make_async_copy(rows, rows, recv_sem.at[h]).wait()

    def batch(first, count):
        for t in range(count):
            r_stage[first + t] = score(first + t)

    def next_keys(b):
        rows = k_all.at[pl.ds(b * BATCH, BATCH)]
        pltpu.make_async_copy(rows, rows, k_recv.at[b]).wait()
        key_rows(b).start()

    key_rows(0).wait()
    arrived(1, HALF - 1, 0)
    next_keys(1)
    batch(0, HALF)
    arrived(HALF, HALF, 1)
    batch(HALF, HALF)
    r_recv[0] = r_stage[0]
    for j in range(1, BATCH):
        back(j)

    pp_load.wait()

    pltpu.make_async_copy(all_qp.at[pl.ds(0, 15)], all_qp.at[pl.ds(0, 15)], qp_recv).wait()
    scores = lax.dot_general(
        pp_ref[...], all_qp[...].reshape(256, 256), (((1,), (1,)), ((), ())),
        preferred_element_type=jnp.float32,
    )
    best = jnp.concatenate(
        [jnp.max(scores[c * CSIZE : (c + 1) * CSIZE], axis=0, keepdims=True) for c in range(4)], axis=0
    )
    c_stage[0] = best[:, :128]
    c_stage[1] = best[:, 128:]
    c_recv[s] = c_stage[lax.div(s, 8)]
    for j in SHARD_MATES:
        to = ahead(j)
        pltpu.make_async_remote_copy(
            c_stage.at[lax.div(to[1], 8)], c_recv.at[s], c_send, c_rsem, to, MESH
        ).start()

    @pl.loop(1, N_BATCH - 1)
    def _(b):
        first = b * BATCH
        arrived(first, HALF, 2 * b)
        arrived(first + HALF, HALF, 2 * b + 1)
        next_keys(b + 1)
        key_rows(b).wait()
        batch(first, BATCH)
        for n in range(1, N_BATCH - 1):

            @pl.when(b == n)
            def _():
                for j in range(n * BATCH, (n + 1) * BATCH):
                    back(j)

    key_rows(N_BATCH - 1).wait()

    @pl.loop(2 * N_BATCH - 2, 2 * N_BATCH)
    def _(h):
        arrived(h * HALF, HALF, h)
        batch(h * HALF, HALF)
        for n in (2 * N_BATCH - 2, 2 * N_BATCH - 1):

            @pl.when(h == n)
            def _():
                for j in range(n * HALF, (n + 1) * HALF):
                    back(j)

    row8 = lax.broadcasted_iota(jnp.int32, (8, 16), 0)

    def across(column):
        return jnp.sum(jnp.where(eye, column, 0.0), axis=0, keepdims=True)


    pltpu.make_async_copy(c_recv.at[pl.ds(0, 15)], c_recv.at[pl.ds(0, 15)], c_rsem).wait()
    probes_load.wait()
    all_best = c_recv[...]
    cluster = 4 * lax.broadcasted_iota(jnp.int32, (16, 4, 128), 0) + lax.broadcasted_iota(
        jnp.int32, (16, 4, 128), 1
    )
    first_lane = lax.rem(s, 8) * 16
    probes = jnp.concatenate([probes_ref[...], jnp.zeros((8, 112), jnp.int32)], axis=1)
    probes = pltpu.roll(probes, first_lane, 1)
    row_k = lax.broadcasted_iota(jnp.int32, (8, 128), 0)
    out = jnp.zeros((8, 128), jnp.float32)
    for k in range(8):
        hit = probes[k : k + 1][None] == cluster
        pick = jnp.sum(jnp.sum(jnp.where(hit, all_best, 0.0), axis=0), axis=0, keepdims=True)
        out = jnp.where(row_k == k, pick, out)
    out = pltpu.roll(out, lax.rem(128 - first_lane, 128), 1)[:, :16]
    out_ref[0] = out

    pltpu.make_async_copy(r_recv.at[pl.ds(1, 127)], r_recv.at[pl.ds(1, 127)], r_rsem).wait()
    both = jnp.sum(r_recv[...], axis=0)
    out = jnp.zeros((8, 16), jnp.float32)
    for k in range(8):
        here = (cand[k] >> 8) == lane
        value = jnp.where(first_flat == row * 8 + k, both[0:1], both[1:2])
        pick = jnp.sum(jnp.where(here, value, 0.0), axis=1, keepdims=True)
        out = jnp.where(row8 == k, across(pick), out)
    out_ref[1] = out

    def sent(ref, sem):
        pltpu.make_async_copy(ref, ref, sem).wait()

    sent(stage.at[pl.ds(1, 127)], send_sem)
    sent(all_qp.at[pl.ds(0, 15)], qp_send)
    sent(k_all.at[pl.ds(1, 127)], k_send)
    sent(c_recv.at[pl.ds(0, 15)], c_send)
    sent(r_stage.at[pl.ds(1, 127)], r_send)


def body(query_prefix, query_tokens, probes, candidates, passage_prefix, passage_tokens):
    vmem = pl.BlockSpec(memory_space=pltpu.VMEM)
    dma = pltpu.SemaphoreType.DMA
    scores = (
        pl.pallas_call(
            kernel,
            out_shape=jax.ShapeDtypeStruct((2, 8, 16), jnp.float32),
            in_specs=[pl.BlockSpec(memory_space=pltpu.HBM)] * 6,
            out_specs=vmem,
            scratch_shapes=[
                pltpu.VMEM((16, 256), jnp.bfloat16),
                pltpu.VMEM((16, 32, 128), jnp.bfloat16),
                pltpu.VMEM((8, 16), jnp.int32),
                pltpu.VMEM((8, 16), jnp.int32),
                pltpu.VMEM((256, 256), jnp.bfloat16),
                pltpu.VMEM((256, 128, 128), jnp.bfloat16),
                pltpu.VMEM((N_DEV, 2, 32, 128), jnp.bfloat16),
                pltpu.VMEM((N_DEV, 2, 32, 128), jnp.bfloat16),
                pltpu.VMEM((16, 16, 256), jnp.bfloat16),
                pltpu.VMEM((2, 4, 128), jnp.float32),
                pltpu.VMEM((16, 4, 128), jnp.float32),
                pltpu.VMEM((1, 128), jnp.int32),
                pltpu.VMEM((1, 128), jnp.int32),
                pltpu.VMEM((N_DEV, 1, 128), jnp.int32),
                pltpu.VMEM((N_DEV, 2, 128), jnp.float32),
                pltpu.VMEM((N_DEV, 2, 128), jnp.float32),
                pltpu.SMEM((1, 128), jnp.int32),
                pltpu.SMEM((N_DEV, 1, 128), jnp.int32),
                dma((6,)), dma, dma((N_BATCH,)), pltpu.SemaphoreType.REGULAR,
                dma, dma((2 * N_BATCH,)), dma, dma, dma, dma((N_BATCH,)), dma, dma, dma, dma,
            ],
            compiler_params=pltpu.CompilerParams(
                collective_id=0, has_side_effects=True, vmem_limit_bytes=60 * 1024 * 1024
            ),
            cost_estimate=pl.CostEstimate(
                flops=300_000_000, bytes_accessed=8_700_000, transcendentals=0
            ),
        )(query_prefix, query_tokens, probes.T, candidates.T, passage_prefix, passage_tokens)
    )
    return scores[0].T, scores[1].T


def solution(mesh):
    both = ("group", "shard")
    flat, cube = P(both, None), P(both, None, None)
    return jax.shard_map(
        body,
        mesh=mesh,
        in_specs=(flat, cube, flat, flat, flat, cube),
        out_specs=(flat, flat),
        check_vma=False,
    )
```
